512 devices in a mesh: seq: 128 (over x, z, core), head: 4 (over y).
Axes of the slice: x: 4, y: 4, z: 16, core: 2. Of those that a mesh axis runs over, the one named last changes fastest.
Arguments:
- queries: bfloat16 [32768, 2048], P('seq', 'head'), may hold values from -10 to 10
- keys: bfloat16 [32768, 2048], P('seq', 'head'), may hold values from -10 to 10
- values: bfloat16 [32768, 2048], P('seq', 'head'), may hold values from -6 to 6
- out_grad: bfloat16 [32768, 2048], P('seq', 'head'), may hold values from -6 to 6
- cluster_ids: int32 [32768, 2], P('seq'), may hold values from 0 to 255, as said below
- slots: int32 [32768, 2], P('seq'), may hold values from 0 to 255, as said below
Outputs:
- attn_out: bfloat16 [32768, 2048], P('seq', 'head')
- grad_q: bfloat16 [32768, 2048], P('seq', 'head')
- grad_k: bfloat16 [32768, 2048], P('seq', 'head')
- grad_v: bfloat16 [32768, 2048], P('seq', 'head')
- cluster_means: float32 [256, 128], P('seq')
The draws below stay inside these ranges and needn't reach their ends.
Inputs may be any that keep to these rules, and one draw needn't show every extreme that they name: `cluster_ids`: each cluster is named by exactly 256 of the 65536 ids, and a token's two ids differ. Clusters o * 2 to (o + 1) * 2 - 1 form group o. Of the 512 ids of each aligned block of 256 tokens, at most 8 name clusters of one group, and every block has a group that receives exactly 8 of them. The 256 members of each cluster hold the slots 0 to 255, each once, rising with the token index.
All inputs are finite; a program needn't handle non-finite values.
Results may differ from the reference program's by a relative error of at most 0.0094.
Values may be sent and summed in bfloat16 or wider, within the bound.
A program may use at most 64 MiB of HBM per device.

```python
import math
import jax
import jax.numpy as jnp
from jax import lax

HEADS = 16
HEAD_DIM = 128
CLUSTER_SIZE = 256
TOK_DEV = 256
TOKENS = 32768
CLUSTERS = 256
N_SEQ = 128


def route_tables(key):
    cap_one = 2 * TOK_DEV // N_SEQ
    per_block = TOK_DEV // CLUSTER_SIZE
    local_count = 2 * per_block
    subkeys = jax.random.split(key, 6)
    owner_order = jax.random.permutation(subkeys[0], N_SEQ).astype(jnp.int32)
    source = jnp.arange(N_SEQ, dtype=jnp.int32)[:, None]
    lag_index = (jnp.arange(N_SEQ, dtype=jnp.int32)[:, None] - jnp.arange(N_SEQ, dtype=jnp.int32)[None, :]) % N_SEQ
    rotation = jax.random.randint(subkeys[5], (N_SEQ,), 0, local_count).astype(jnp.int32)
    id_list = []
    slot_list = []
    for copy_index in range(2):
        halves = jax.random.randint(subkeys[1 + copy_index], (N_SEQ // 2,), 0, cap_one + 1).astype(jnp.int32)
        halves = halves.at[0].set(cap_one)
        counts = jnp.stack([halves, cap_one - halves], axis=1).reshape(N_SEQ)
        bounds = jnp.cumsum(counts)

        def shuffle_one(subkey):
            return jax.random.permutation(subkey, TOK_DEV).astype(jnp.int32)
        token_rank = jax.vmap(shuffle_one)(jax.random.split(subkeys[3 + copy_index], N_SEQ))
        stride = jnp.searchsorted(bounds, token_rank, side='right').astype(jnp.int32)
        stride_hits = (stride[:, :, None] == jnp.arange(N_SEQ, dtype=jnp.int32)[None, None, :]).astype(jnp.int32)
        earlier = jnp.cumsum(stride_hits, axis=1) - stride_hits
        within = jnp.sum(earlier * stride_hits, axis=2)
        column = (source + stride) % N_SEQ
        owner_index = owner_order[column]
        lagged = counts[lag_index]
        before = jnp.cumsum(lagged, axis=1) - lagged
        arrival = before[column, jnp.broadcast_to(source, column.shape)] + within
        local_index = copy_index * per_block + arrival // CLUSTER_SIZE
        cluster = owner_index * local_count + (local_index + rotation[owner_index]) % local_count
        id_list.append(cluster.reshape(TOKENS))
        slot_list.append((arrival % CLUSTER_SIZE).reshape(TOKENS))
    return (jnp.stack(id_list, axis=1).astype(jnp.int32), jnp.stack(slot_list, axis=1).astype(jnp.int32))


def draw_cluster_ids(key, part):
    return route_tables(key)[0]


def draw_slots(key, part):
    return route_tables(key)[1]


def draw_queries(key, part):
    key = jax.random.fold_in(key, 11)
    noise_key = jax.random.fold_in(key, 0)
    raw_rows = jax.random.normal(noise_key, (TOKENS, HEADS, HEAD_DIM), jnp.float32)
    return jnp.clip(raw_rows, -10.0, 10.0).reshape(TOKENS, HEADS * HEAD_DIM).astype(jnp.bfloat16)


def draw_keys(key, part):
    key = jax.random.fold_in(key, 23)
    noise_key = jax.random.fold_in(key, 0)
    raw_rows = jax.random.normal(noise_key, (TOKENS, HEADS, HEAD_DIM), jnp.float32)
    return jnp.clip(raw_rows, -10.0, 10.0).reshape(TOKENS, HEADS * HEAD_DIM).astype(jnp.bfloat16)


def block_scale(own_key, shape, cuts, low, top_value):
    def one(position, parts):
        heights = jax.random.uniform(jax.random.fold_in(jax.random.fold_in(own_key, 6), position), (parts,), jnp.float32, low / len(cuts), top_value / len(cuts))
        return jnp.repeat(jnp.exp(heights), shape[position] // parts).reshape((-1,) + (1,) * (len(shape) - position - 1))

    level = one(*cuts[0])
    for cut in cuts[1:]:
        level = level * one(*cut)
    return level


def bell_draw(stream_key, shape, scale, reach, cuts=(), kind=jnp.bfloat16):
    drawn = jax.random.normal(stream_key, shape, jnp.float32) * scale
    if len(cuts) > 0:
        drawn = block_scale(stream_key, shape, cuts, -0.22, 0.18) * drawn
    return jnp.clip(drawn, min=-reach, max=reach).astype(kind)


def setup_inputs(seed: int = 0) -> dict:
    arg_keys = jax.random.split(jax.random.key(seed), 7)
    queries = draw_queries(jax.random.fold_in(arg_keys[6], 71), 0)
    keys = draw_keys(jax.random.fold_in(arg_keys[6], 71), 0)
    values = bell_draw(arg_keys[2], (TOKENS, HEADS * HEAD_DIM), 1.0, 6.0, ((0, 128), (1, 4)))
    out_grad = bell_draw(arg_keys[3], (TOKENS, HEADS * HEAD_DIM), 1.0, 6.0, ((0, 128), (1, 4)))
    cluster_ids = draw_cluster_ids(jax.random.fold_in(arg_keys[6], 71), 0)
    slots = draw_slots(jax.random.fold_in(arg_keys[6], 71), 0)
    return {"queries": queries, "keys": keys, "values": values, "out_grad": out_grad, "cluster_ids": cluster_ids, "slots": slots}


def reference(queries, keys, values, out_grad, cluster_ids, slots):
    total_tokens = queries.shape[0]
    score_scale = 1.0 / math.sqrt(HEAD_DIM)
    flat_index = (cluster_ids * CLUSTER_SIZE + slots).astype(jnp.int32)
    token_index = jnp.repeat(jnp.arange(total_tokens, dtype=jnp.int32), 2)
    members = jnp.zeros((CLUSTERS * CLUSTER_SIZE,), jnp.int32).at[flat_index.reshape(-1)].set(token_index)
    members = members.reshape(CLUSTERS, CLUSTER_SIZE)
    slot_order = jnp.arange(CLUSTER_SIZE, dtype=jnp.int32)
    allowed = slot_order[None, :] <= slot_order[:, None]

    def one_cluster(member_index):

        def rows_of(source):
            return source[member_index].astype(jnp.float32).reshape(CLUSTER_SIZE, HEADS, HEAD_DIM)
        query_rows = rows_of(queries)
        key_rows = rows_of(keys)
        value_rows = rows_of(values)
        grad_rows = rows_of(out_grad)
        scores = jnp.einsum('qhd,khd->hqk', query_rows, key_rows) * score_scale
        scores = jnp.where(allowed[None, :, :], scores, jnp.float32(-1e+30))
        row_max = lax.optimization_barrier(jnp.max(scores, axis=2, keepdims=True))
        weights = jnp.exp(scores - row_max)
        attention = weights / lax.optimization_barrier(jnp.sum(weights, axis=2, keepdims=True))
        attn_low = lax.optimization_barrier(attention.astype(jnp.bfloat16)).astype(jnp.float32)
        attended = jnp.einsum('hqk,khd->qhd', attn_low, value_rows)
        prob_grad = jnp.einsum('qhd,khd->hqk', grad_rows, value_rows)
        row_dot = lax.optimization_barrier(jnp.sum(attention * prob_grad, axis=2, keepdims=True))
        grad_score = (attention * (prob_grad - row_dot) * score_scale).astype(jnp.bfloat16)
        grad_score = lax.optimization_barrier(grad_score).astype(jnp.float32)
        grad_query = jnp.einsum('hqk,khd->qhd', grad_score, key_rows)
        grad_key = jnp.einsum('hqk,qhd->khd', grad_score, query_rows)
        grad_value = jnp.einsum('hqk,qhd->khd', attn_low, grad_rows)
        normed = key_rows * lax.rsqrt(lax.optimization_barrier(jnp.mean(key_rows * key_rows, axis=2, keepdims=True)) + 1e-06)
        centroid = lax.optimization_barrier(jnp.sum(normed, axis=(0, 1)))

        def flatten(result):
            return result.reshape(CLUSTER_SIZE, HEADS * HEAD_DIM).astype(jnp.bfloat16)
        return (flatten(attended), flatten(grad_query), flatten(grad_key), flatten(grad_value), centroid)
    results = lax.map(one_cluster, members)

    def combine(stacked):
        rows_all = stacked.reshape(CLUSTERS * CLUSTER_SIZE, HEADS * HEAD_DIM)
        first_copy = rows_all[flat_index[:, 0]].astype(jnp.float32)
        second_copy = rows_all[flat_index[:, 1]].astype(jnp.float32)
        return (first_copy + second_copy).astype(jnp.bfloat16)
    sums = results[4]
    means = sums * lax.rsqrt(lax.optimization_barrier(jnp.mean(sums * sums, axis=1, keepdims=True)) + 1e-06)
    return (combine(results[0]), combine(results[1]), combine(results[2]), combine(results[3]), means)
```

```python
import functools
import math

import jax
import jax.numpy as jnp
from jax import lax
from jax.experimental import pallas as pl
from jax.experimental.pallas import tpu as pltpu
from jax.sharding import PartitionSpec as P

HEAD_DIM = 128
CLUSTER_SIZE = 256


def attend(query_rows, key_rows, value_rows, score_scale):
    scores = (
        jnp.einsum("cqhd,ckhd->chqk", query_rows, key_rows, preferred_element_type=jnp.float32)
        * score_scale
    )
    slot_order = jnp.arange(query_rows.shape[1], dtype=jnp.int32)
    allowed = slot_order[None, :] <= slot_order[:, None]
    scores = jnp.where(allowed, scores, jnp.float32(-1e30))
    row_max = jnp.max(scores, axis=3, keepdims=True)
    weights = jnp.exp(scores - row_max)
    attention = weights / jnp.sum(weights, axis=3, keepdims=True)
    attn_low = attention.astype(jnp.bfloat16)
    attended = jnp.einsum(
        "chqk,ckhd->cqhd", attn_low, value_rows, preferred_element_type=jnp.float32
    )
    return (attention, attn_low, attended.astype(jnp.bfloat16))


def backprop(query_rows, key_rows, value_rows, grad_rows, attention, attn_low, score_scale):
    prob_grad = jnp.einsum(
        "cqhd,ckhd->chqk", grad_rows, value_rows, preferred_element_type=jnp.float32
    )
    row_dot = jnp.sum(attention * prob_grad, axis=3, keepdims=True)
    grad_score = (attention * (prob_grad - row_dot) * score_scale).astype(jnp.bfloat16)
    grad_query = jnp.einsum(
        "chqk,ckhd->cqhd", grad_score, key_rows, preferred_element_type=jnp.float32
    )
    grad_key = jnp.einsum(
        "chqk,cqhd->ckhd", grad_score, query_rows, preferred_element_type=jnp.float32
    )
    grad_value = jnp.einsum(
        "chqk,cqhd->ckhd", attn_low, grad_rows, preferred_element_type=jnp.float32
    )
    return (
        grad_query.astype(jnp.bfloat16),
        grad_key.astype(jnp.bfloat16),
        grad_value.astype(jnp.bfloat16),
    )


def key_centroids(key_rows):
    key_float = key_rows.astype(jnp.float32)
    normed = key_float * lax.rsqrt(jnp.mean(key_float * key_float, axis=3, keepdims=True) + 1e-06)
    return jnp.sum(normed, axis=(1, 2))


def exchange_kernel(shards, send_ref, out_ref, send_sem, recv_sem, own_sem):
    me = lax.axis_index("seq")
    head = lax.axis_index("head")
    barrier = pltpu.get_barrier_semaphore()

    def greet(step, carry):
        peer = lax.rem(me + step, shards)
        pl.semaphore_signal(
            barrier, inc=1, device_id=(peer, head), device_id_type=pl.DeviceIdType.MESH
        )
        return carry

    lax.fori_loop(1, shards, greet, 0)
    own = pltpu.make_async_copy(send_ref.at[me], out_ref.at[me], own_sem)
    own.start()
    pl.semaphore_wait(barrier, shards - 1)

    def send(step, carry):
        peer = lax.rem(me + step, shards)
        pltpu.make_async_remote_copy(
            src_ref=send_ref.at[peer],
            dst_ref=out_ref.at[me],
            send_sem=send_sem,
            recv_sem=recv_sem,
            device_id=(peer, head),
            device_id_type=pl.DeviceIdType.MESH,
        ).start()
        return carry

    lax.fori_loop(1, shards, send, 0)
    own.wait()
    whole = pltpu.make_async_remote_copy(
        src_ref=send_ref.at[pl.ds(0, shards - 1)],
        dst_ref=out_ref.at[pl.ds(0, shards - 1)],
        send_sem=send_sem,
        recv_sem=recv_sem,
        device_id=(lax.rem(me + 1, shards), head),
        device_id_type=pl.DeviceIdType.MESH,
    )
    whole.wait_send()
    whole.wait_recv()


def exchange(boxes, collective_id):
    shards = boxes.shape[0]
    return pl.pallas_call(
        functools.partial(exchange_kernel, shards),
        out_shape=jax.ShapeDtypeStruct(boxes.shape, boxes.dtype),
        in_specs=[pl.BlockSpec(memory_space=pltpu.VMEM)],
        out_specs=pl.BlockSpec(memory_space=pltpu.VMEM),
        scratch_shapes=[
            pltpu.SemaphoreType.DMA,
            pltpu.SemaphoreType.DMA,
            pltpu.SemaphoreType.DMA,
        ],
        compiler_params=pltpu.CompilerParams(
            collective_id=collective_id, has_side_effects=True, vmem_limit_bytes=24 * 2**20
        ),
    )(boxes)


def local(queries, keys, values, out_grad, cluster_ids, slots):
    tok_rows = queries.shape[0]
    row_width = queries.shape[1]
    head_count = row_width // HEAD_DIM
    shards = lax.axis_size("seq")
    capacity = 4 * tok_rows // shards
    buffer_rows = shards * capacity
    clusters_here = 2 * tok_rows // CLUSTER_SIZE
    cluster_rows = clusters_here * CLUSTER_SIZE
    score_scale = 1.0 / math.sqrt(HEAD_DIM)
    owners = (cluster_ids // clusters_here).reshape(-1)
    owner_hits = (owners[:, None] == jnp.arange(shards, dtype=jnp.int32)[None, :]).astype(jnp.int32)
    earlier = jnp.cumsum(owner_hits, axis=0) - owner_hits
    buffer_slot = owners * capacity + jnp.sum(earlier * owner_hits, axis=1)
    targets = (cluster_ids % clusters_here * CLUSTER_SIZE + slots).reshape(-1)
    routing = jnp.full((buffer_rows,), -1, jnp.int32).at[buffer_slot].set(targets)
    slot_hits = buffer_slot[None, :] == jnp.arange(buffer_rows, dtype=jnp.int32)[:, None]
    dispatch = jnp.any(slot_hits.reshape(buffer_rows, tok_rows, 2), axis=2).astype(jnp.bfloat16)

    def pack_rows(rows_in):
        return jnp.dot(dispatch, rows_in, preferred_element_type=jnp.float32).astype(jnp.bfloat16)

    def unpack_rows(rows_in):
        summed = lax.dot_general(
            dispatch, rows_in, (((0,), (0,)), ((), ())), preferred_element_type=jnp.float32
        )
        return summed.astype(jnp.bfloat16)

    routing_in = lax.all_to_all(routing, "seq", split_axis=0, concat_axis=0, tiled=True)

    def box(rows_in):
        return rows_in.reshape(shards, capacity, row_width)

    def unbox(boxes, index):
        part = boxes[:, index * capacity : (index + 1) * capacity]
        return part.reshape(buffer_rows, row_width)

    arrived = exchange(
        jnp.concatenate([box(pack_rows(a)) for a in (queries, keys, values, out_grad)], axis=1), 0
    )
    sent_query, sent_key, sent_value, sent_grad = (unbox(arrived, i) for i in range(4))
    gather_table = (
        routing_in[None, :] == jnp.arange(cluster_rows, dtype=jnp.int32)[:, None]
    ).astype(jnp.bfloat16)

    def gather_rows(rows_in):
        grouped = jnp.dot(gather_table, rows_in, preferred_element_type=jnp.float32).astype(
            jnp.bfloat16
        )
        return grouped.reshape(clusters_here, CLUSTER_SIZE, head_count, HEAD_DIM)

    def scatter_rows(grouped):
        flat_rows = grouped.reshape(cluster_rows, row_width)
        spread = lax.dot_general(
            gather_table, flat_rows, (((0,), (0,)), ((), ())), preferred_element_type=jnp.float32
        )
        return spread.astype(jnp.bfloat16)

    query_rows = gather_rows(sent_query)
    key_rows = gather_rows(sent_key)
    value_rows = gather_rows(sent_value)
    attention, attn_low, attended = attend(query_rows, key_rows, value_rows, score_scale)
    totals = lax.psum(key_centroids(key_rows), "head")
    cluster_means = totals * lax.rsqrt(jnp.mean(totals * totals, axis=1, keepdims=True) + 1e-06)
    grad_rows = gather_rows(sent_grad)
    grad_query, grad_key, grad_value = backprop(
        query_rows, key_rows, value_rows, grad_rows, attention, attn_low, score_scale
    )
    returned = exchange(
        jnp.concatenate(
            [box(scatter_rows(a)) for a in (attended, grad_query, grad_key, grad_value)], axis=1
        ),
        1,
    )
    back_out, back_query, back_key, back_value = (unbox(returned, i) for i in range(4))
    return (
        unpack_rows(back_out),
        unpack_rows(back_query),
        unpack_rows(back_key),
        unpack_rows(back_value),
        cluster_means,
    )


def solution(mesh):
    placed = (
        P("seq", "head"),
        P("seq", "head"),
        P("seq", "head"),
        P("seq", "head"),
        P("seq", None),
        P("seq", None),
    )
    return jax.shard_map(
        local,
        mesh=mesh,
        in_specs=placed,
        out_specs=(
            P("seq", "head"),
            P("seq", "head"),
            P("seq", "head"),
            P("seq", "head"),
            P("seq", None),
        ),
        check_vma=False,
    )
```

```python
import functools
import math

import jax
import jax.numpy as jnp
from jax import lax
from jax.experimental import pallas as pl
from jax.experimental.pallas import tpu as pltpu
from jax.sharding import PartitionSpec as P

HEAD_DIM = 128
CLUSTER_SIZE = 256
RING = 16
PLANE = 8
REACH = 4
MESH = pl.DeviceIdType.MESH


def far_planes(way, pair):
    return 4 if way == pair else 3


def place():
    me = lax.axis_index("seq")
    head = lax.axis_index("head")
    return (me, head, me // (2 * RING), lax.rem(me // 2, RING), lax.rem(me, 2))


def device_at(column, height, core):
    return (column * RING + lax.rem(height + RING, RING)) * 2 + core


def greet_all(me, head, shards):
    barrier = pltpu.get_barrier_semaphore()

    def greet(step, carry):
        peer = lax.rem(me + step, shards)
        pl.semaphore_signal(barrier, inc=1, device_id=(peer, head), device_id_type=MESH)
        return carry

    lax.fori_loop(1, shards, greet, 0)
    return barrier


def hit_table(slot_rows, height):
    rows, lanes = (2 * PLANE * 8, slot_rows.shape[1])
    row = lax.broadcasted_iota(jnp.int32, (rows, lanes), 0)
    lane = lax.broadcasted_iota(jnp.int32, (rows, lanes), 1)
    group = device_at(row // 32, height, row // 16 % 2)
    wanted = group * 8 + row % 8
    hit = (slot_rows[0:1, :] == wanted) | (slot_rows[1:2, :] == wanted)
    same = row // 8 % 2 == lane // (lanes // 2)
    return jnp.where(hit & same, 1.0, 0.0).astype(jnp.bfloat16)


def spread_kernel(
    shards, rows_ref, slots_ref, targets_ref, boxes_ref, held_slots_ref, held_targets_ref,
    passing, near_box, far_box, slot_send, slot_recv, target_send, target_recv,
    pass_send, pass_recv, box_send, box_recv, own_sem,
):
    me, head, column, height, core = place()
    mine = column * 2 + core
    barrier = greet_all(me, head, shards)
    held_slots_ref[2 * REACH] = slots_ref[...]
    held_targets_ref[me] = targets_ref[me]
    pl.semaphore_wait(barrier, shards - 1)

    def slot_copy(way, hop):
        step = hop if way == 0 else -hop
        return pltpu.make_async_remote_copy(
            src_ref=slots_ref,
            dst_ref=held_slots_ref.at[way * REACH + hop - 1],
            send_sem=slot_send,
            recv_sem=slot_recv,
            device_id=(device_at(column, height + step, core), head),
            device_id_type=MESH,
        )

    def pass_on(way, hop, pair):
        step = 1 if way == 0 else -1
        source = rows_ref.at[pair] if hop == 0 else passing.at[way, hop - 1, pair]
        return pltpu.make_async_remote_copy(
            src_ref=source,
            dst_ref=passing.at[way, hop, pair],
            send_sem=pass_send.at[way, hop, pair],
            recv_sem=pass_recv.at[way, hop, pair],
            device_id=(device_at(column, height + step, core), head),
            device_id_type=MESH,
        )

    def box_copy(source, block, pair, place_to):
        return pltpu.make_async_remote_copy(
            src_ref=source,
            dst_ref=boxes_ref.at[block, pair],
            send_sem=box_send,
            recv_sem=box_recv,
            device_id=(place_to, head),
            device_id_type=MESH,
        )

    for way in range(2):
        for hop in range(1, REACH + 1):
            slot_copy(way, hop).start()
    for pair in range(2):
        for way in range(2):
            pass_on(way, 0, pair).start()

    def send_target(step, carry):
        peer = lax.rem(me + step, shards)
        pltpu.make_async_remote_copy(
            src_ref=targets_ref.at[peer],
            dst_ref=held_targets_ref.at[me],
            send_sem=target_send,
            recv_sem=target_recv,
            device_id=(peer, head),
            device_id_type=MESH,
        ).start()
        return carry

    lax.fori_loop(1, shards, send_target, 0)

    def deliver_near(block_rows, slot_rows, block_height, index, pair):
        table = hit_table(slot_rows, height)
        packed = jnp.dot(table, block_rows, preferred_element_type=jnp.float32)
        near_box[index, pair] = packed.astype(jnp.bfloat16).reshape(PLANE, 16, -1)
        block = device_at(column, block_height, core)
        pltpu.make_async_copy(
            near_box.at[index, pair, mine], boxes_ref.at[block, pair], own_sem
        ).start()

        def send(step, carry):
            peer = lax.rem(mine + step, PLANE)
            box_copy(
                near_box.at[index, pair, peer], block, pair,
                device_at(peer // 2, height, lax.rem(peer, 2)),
            ).start()
            return carry

        lax.fori_loop(1, PLANE, send, 0)

    def deliver_far(block_rows, slot_rows, way, pair):
        sign = 1 if way == 0 else -1
        block = device_at(column, height - sign * REACH, core)
        for away in range(far_planes(way, pair), 0, -1):
            there = height + sign * away
            table = hit_table(slot_rows, there)
            packed = jnp.dot(table, block_rows, preferred_element_type=jnp.float32)
            far_box[way, pair, away - 1] = packed.astype(jnp.bfloat16).reshape(PLANE, 16, -1)

            def send(step, carry):
                peer = lax.rem(mine + step, PLANE)
                box_copy(
                    far_box.at[way, pair, away - 1, peer], block, pair,
                    device_at(peer // 2, there, lax.rem(peer, 2)),
                ).start()
                return carry

            lax.fori_loop(0, PLANE, send, 0)

    for pair in range(2):
        deliver_near(rows_ref[pair], slots_ref[...], height, 2 * REACH, pair)
    every = pltpu.make_async_remote_copy(
        src_ref=held_slots_ref.at[pl.ds(0, 2 * REACH)],
        dst_ref=held_slots_ref.at[pl.ds(0, 2 * REACH)],
        send_sem=slot_send,
        recv_sem=slot_recv,
        device_id=(device_at(column, height + 1, core), head),
        device_id_type=MESH,
    )
    every.wait_send()
    every.wait_recv()
    for hop in range(1, REACH + 1):
        for pair in range(2):
            for way in range(2):
                pass_on(way, hop - 1, pair).wait_recv()
                if hop < REACH:
                    pass_on(way, hop, pair).start()
                index = way * REACH + hop - 1
                block_rows = passing[way, hop - 1, pair]
                if hop == REACH:
                    deliver_far(block_rows, held_slots_ref[index], way, pair)
                block_height = height - hop if way == 0 else height + hop
                deliver_near(block_rows, held_slots_ref[index], block_height, index, pair)
    for hop in range(REACH):
        for pair in range(2):
            for way in range(2):
                pass_on(way, hop, pair).wait_send()
    for index in range(2 * REACH + 1):
        for pair in range(2):
            pltpu.make_async_copy(
                near_box.at[index, pair, mine], boxes_ref.at[0, pair], own_sem
            ).wait()
    remote = shards - (2 * REACH + 1)
    lot = pltpu.make_async_remote_copy(
        src_ref=boxes_ref.at[pl.ds(0, remote)],
        dst_ref=boxes_ref.at[pl.ds(0, remote)],
        send_sem=box_send,
        recv_sem=box_recv,
        device_id=(device_at(column, height + 1, core), head),
        device_id_type=MESH,
    )
    lot.wait_send()
    lot.wait_recv()
    lines = pltpu.make_async_remote_copy(
        src_ref=targets_ref.at[pl.ds(0, shards - 1)],
        dst_ref=held_targets_ref.at[pl.ds(0, shards - 1)],
        send_sem=target_send,
        recv_sem=target_recv,
        device_id=(device_at(column, height + 1, core), head),
        device_id_type=MESH,
    )
    lines.wait_send()
    lines.wait_recv()


def spread(rows, slots, targets):
    shards = targets.shape[0]
    _, count, width = rows.shape
    vmem = pl.BlockSpec(memory_space=pltpu.VMEM)
    dma = pltpu.SemaphoreType.DMA
    return pl.pallas_call(
        functools.partial(spread_kernel, shards),
        out_shape=(
            jax.ShapeDtypeStruct((shards, 2, 16, width), jnp.bfloat16),
            jax.ShapeDtypeStruct((2 * REACH + 1,) + slots.shape, jnp.int32),
            jax.ShapeDtypeStruct(targets.shape, jnp.int32),
        ),
        in_specs=[vmem] * 3,
        out_specs=(vmem,) * 3,
        scratch_shapes=[
            pltpu.VMEM((2, REACH, 2, count, width), jnp.bfloat16),
            pltpu.VMEM((2 * REACH + 1, 2, PLANE, 16, width), jnp.bfloat16),
            pltpu.VMEM((2, 2, 4, PLANE, 16, width), jnp.bfloat16),
            dma, dma, dma, dma,
            dma((2, REACH, 2)), dma((2, REACH, 2)),
            dma, dma, dma,
        ],
        compiler_params=pltpu.CompilerParams(
            collective_id=0, has_side_effects=True, vmem_limit_bytes=48 * 2**20
        ),
    )(rows, slots, targets)


def collect_kernel(
    shards, boxes_ref, held_slots_ref, sums_ref, rows_ref, totals_ref,
    passing, near_box, far_box, sums, pass_send, pass_recv, near_send, near_recv, own_sem,
    far_send, far_recv, sum_send, sum_recv,
):
    me, head, column, height, core = place()
    mine = column * 2 + core
    heads = sums.shape[0]
    barrier = greet_all(me, head, shards)

    def other_head(step):
        return (me, lax.rem(head + step, heads))

    for step in range(1, heads):
        pl.semaphore_signal(barrier, inc=1, device_id=other_head(step), device_id_type=MESH)
    sums[head] = sums_ref[...]
    pl.semaphore_wait(barrier, shards - 1 + heads - 1)

    def pass_on(way, hop, pair):
        step = -1 if way == 0 else 1
        return pltpu.make_async_remote_copy(
            src_ref=passing.at[way, hop, pair],
            dst_ref=passing.at[way, hop - 1, pair],
            send_sem=pass_send.at[way, hop - 1, pair],
            recv_sem=pass_recv.at[way, hop - 1, pair],
            device_id=(device_at(column, height + step, core), head),
            device_id_type=MESH,
        )

    for pair in range(2):
        for way in range(2):
            sign = 1 if way == 0 else -1
            for away in range(far_planes(way, pair), 0, -1):

                def send_far(step, carry):
                    peer = lax.rem(mine + step, PLANE)
                    block = device_at(
                        peer // 2, height - sign * (REACH + away), lax.rem(peer, 2)
                    )
                    relay = device_at(peer // 2, height - sign * away, lax.rem(peer, 2))
                    pltpu.make_async_remote_copy(
                        src_ref=boxes_ref.at[block, pair],
                        dst_ref=far_box.at[way, pair, away - 1, mine],
                        send_sem=far_send.at[way, pair],
                        recv_sem=far_recv.at[way, pair],
                        device_id=(relay, head),
                        device_id_type=MESH,
                    ).start()
                    return carry

                lax.fori_loop(0, PLANE, send_far, 0)
    for step in range(1, heads):
        pltpu.make_async_remote_copy(
            src_ref=sums_ref,
            dst_ref=sums.at[head],
            send_sem=sum_send,
            recv_sem=sum_recv,
            device_id=other_head(step),
            device_id_type=MESH,
        ).start()

    def near_height(index):
        if index == 2 * REACH:
            return height
        hop = index % REACH + 1
        return height - hop if index < REACH else height + hop

    order = [way * REACH + hop - 1 for hop in range(REACH, 0, -1) for way in range(2)]
    for index in order + [2 * REACH]:
        for pair in range(2):
            own = device_at(column, near_height(index), core)
            pltpu.make_async_copy(
                boxes_ref.at[own, pair], near_box.at[index, pair, mine], own_sem.at[index, pair]
            ).start()

            def send_near(step, carry):
                peer = lax.rem(mine + step, PLANE)
                block = device_at(peer // 2, near_height(index), lax.rem(peer, 2))
                pltpu.make_async_remote_copy(
                    src_ref=boxes_ref.at[block, pair],
                    dst_ref=near_box.at[index, pair, mine],
                    send_sem=near_send.at[index, pair],
                    recv_sem=near_recv.at[index, pair],
                    device_id=(device_at(peer // 2, height, lax.rem(peer, 2)), head),
                    device_id_type=MESH,
                ).start()
                return carry

            lax.fori_loop(1, PLANE, send_near, 0)

    def await_near(index, pair):
        pltpu.make_async_copy(
            boxes_ref.at[0, pair], near_box.at[index, pair, 0], own_sem.at[index, pair]
        ).wait()
        lot = near_box.at[index, pair, pl.ds(0, PLANE - 1)]
        copy = pltpu.make_async_remote_copy(
            src_ref=lot,
            dst_ref=lot,
            send_sem=near_send.at[index, pair],
            recv_sem=near_recv.at[index, pair],
            device_id=other_head(1),
            device_id_type=MESH,
        )
        copy.wait_send()
        copy.wait_recv()

    def unpack(slot_rows, there, packed):
        table = hit_table(slot_rows, there)
        return lax.dot_general(
            table, packed.reshape(2 * PLANE * 8, -1), (((0,), (0,)), ((), ())),
            preferred_element_type=jnp.float32,
        )

    for hop in range(REACH, 0, -1):
        for pair in range(2):
            for way in range(2):
                index = way * REACH + hop - 1
                slot_rows = held_slots_ref[index]
                await_near(index, pair)
                total = unpack(slot_rows, height, near_box[index, pair])
                if hop == REACH:
                    planes = far_planes(way, pair)
                    lot = far_box.at[way, pair, pl.ds(0, planes)]
                    copy = pltpu.make_async_remote_copy(
                        src_ref=lot,
                        dst_ref=lot,
                        send_sem=far_send.at[way, pair],
                        recv_sem=far_recv.at[way, pair],
                        device_id=other_head(1),
                        device_id_type=MESH,
                    )
                    copy.wait_send()
                    copy.wait_recv()
                    for away in range(1, planes + 1):
                        there = height + away if way == 0 else height - away
                        total += unpack(slot_rows, there, far_box[way, pair, away - 1])
                else:
                    pass_on(way, hop + 1, pair).wait_recv()
                    total += passing[way, hop, pair].astype(jnp.float32)
                passing[way, hop, pair] = total.astype(jnp.bfloat16)
                pass_on(way, hop, pair).start()
    for pair in range(2):
        await_near(2 * REACH, pair)
        total = unpack(held_slots_ref[2 * REACH], height, near_box[2 * REACH, pair])
        for way in range(2):
            pass_on(way, 1, pair).wait_recv()
            total += passing[way, 0, pair].astype(jnp.float32)
        rows_ref[pair] = total.astype(jnp.bfloat16)
    for hop in range(REACH, 0, -1):
        for pair in range(2):
            for way in range(2):
                pass_on(way, hop, pair).wait_send()
    lines = pltpu.make_async_remote_copy(
        src_ref=sums.at[pl.ds(0, heads - 1)],
        dst_ref=sums.at[pl.ds(0, heads - 1)],
        send_sem=sum_send,
        recv_sem=sum_recv,
        device_id=other_head(1),
        device_id_type=MESH,
    )
    lines.wait_send()
    lines.wait_recv()
    grand = sums[0]
    for step in range(1, heads):
        grand += sums[step]
    totals_ref[...] = grand * lax.rsqrt(jnp.mean(grand * grand, axis=1, keepdims=True) + 1e-06)


def collect(boxes, held_slots, sums):
    shards, _, _, width = boxes.shape
    count = held_slots.shape[2]
    heads = lax.axis_size("head")
    vmem = pl.BlockSpec(memory_space=pltpu.VMEM)
    dma = pltpu.SemaphoreType.DMA
    return pl.pallas_call(
        functools.partial(collect_kernel, shards),
        out_shape=(
            jax.ShapeDtypeStruct((2, count, width), jnp.bfloat16),
            jax.ShapeDtypeStruct(sums.shape, jnp.float32),
        ),
        in_specs=[vmem] * 3,
        out_specs=(vmem,) * 2,
        scratch_shapes=[
            pltpu.VMEM((2, REACH + 1, 2, count, width), jnp.bfloat16),
            pltpu.VMEM((2 * REACH + 1, 2, PLANE, 16, width), jnp.bfloat16),
            pltpu.VMEM((2, 2, 4, PLANE, 16, width), jnp.bfloat16),
            pltpu.VMEM((heads,) + sums.shape, jnp.float32),
            dma((2, REACH, 2)), dma((2, REACH, 2)),
            dma((2 * REACH + 1, 2)), dma((2 * REACH + 1, 2)), dma((2 * REACH + 1, 2)),
            dma((2, 2)), dma((2, 2)), dma, dma,
        ],
        compiler_params=pltpu.CompilerParams(
            collective_id=1, has_side_effects=True, vmem_limit_bytes=48 * 2**20
        ),
    )(boxes, held_slots, sums)


def attend(query_rows, key_rows, value_rows, score_scale):
    scores = (
        jnp.einsum("cqhd,ckhd->chqk", query_rows, key_rows, preferred_element_type=jnp.float32)
        * score_scale
    )
    slot_order = jnp.arange(query_rows.shape[1], dtype=jnp.int32)
    allowed = slot_order[None, :] <= slot_order[:, None]
    scores = jnp.where(allowed, scores, jnp.float32(-1e30))
    row_max = jnp.max(scores, axis=3, keepdims=True)
    weights = jnp.exp(scores - row_max)
    attention = weights / jnp.sum(weights, axis=3, keepdims=True)
    attn_low = attention.astype(jnp.bfloat16)
    attended = jnp.einsum(
        "chqk,ckhd->cqhd", attn_low, value_rows, preferred_element_type=jnp.float32
    )
    return (attention, attn_low, attended.astype(jnp.bfloat16))


def backprop(query_rows, key_rows, value_rows, grad_rows, attention, attn_low, score_scale):
    prob_grad = jnp.einsum(
        "cqhd,ckhd->chqk", grad_rows, value_rows, preferred_element_type=jnp.float32
    )
    row_dot = jnp.sum(attention * prob_grad, axis=3, keepdims=True)
    grad_score = (attention * (prob_grad - row_dot) * score_scale).astype(jnp.bfloat16)
    grad_query = jnp.einsum(
        "chqk,ckhd->cqhd", grad_score, key_rows, preferred_element_type=jnp.float32
    )
    grad_key = jnp.einsum(
        "chqk,cqhd->ckhd", grad_score, query_rows, preferred_element_type=jnp.float32
    )
    grad_value = jnp.einsum(
        "chqk,cqhd->ckhd", attn_low, grad_rows, preferred_element_type=jnp.float32
    )
    return (
        grad_query.astype(jnp.bfloat16),
        grad_key.astype(jnp.bfloat16),
        grad_value.astype(jnp.bfloat16),
    )


def key_centroids(key_rows):
    key_float = key_rows.astype(jnp.float32)
    normed = key_float * lax.rsqrt(jnp.mean(key_float * key_float, axis=3, keepdims=True) + 1e-06)
    return jnp.sum(normed, axis=(1, 2))


def local(queries, keys, values, out_grad, cluster_ids, slots):
    tok_rows = queries.shape[0]
    row_width = queries.shape[1]
    head_count = row_width // HEAD_DIM
    shards = lax.axis_size("seq")
    capacity = 4 * tok_rows // shards
    buffer_rows = shards * capacity
    clusters_here = 2 * tok_rows // CLUSTER_SIZE
    cluster_rows = clusters_here * CLUSTER_SIZE
    score_scale = 1.0 / math.sqrt(HEAD_DIM)
    owners = (cluster_ids // clusters_here).reshape(-1)
    owner_hits = (owners[:, None] == jnp.arange(shards, dtype=jnp.int32)[None, :]).astype(jnp.int32)
    earlier = jnp.cumsum(owner_hits, axis=0) - owner_hits
    buffer_slot = owners * capacity + jnp.sum(earlier * owner_hits, axis=1)
    targets = (cluster_ids % clusters_here * CLUSTER_SIZE + slots).reshape(-1)
    routing = jnp.full((buffer_rows,), -1, jnp.int32).at[buffer_slot].set(targets)
    sent_rows = jnp.concatenate([queries, keys, values, out_grad]).reshape(
        2, 2 * tok_rows, row_width
    )
    copy_slots = buffer_slot.reshape(tok_rows, 2).T
    slot_rows = jnp.pad(jnp.concatenate([copy_slots, copy_slots], axis=1), ((0, 6), (0, 0)))
    target_rows = jnp.pad(routing.reshape(shards, 1, capacity), ((0, 0), (0, 0), (0, 120)))
    arrived, held_slots, held_targets = spread(sent_rows, slot_rows, target_rows)
    routing_in = held_targets[:, 0, :capacity].reshape(-1)

    def unbox(index):
        first = index % 2 * capacity
        return arrived[:, index // 2, first : first + capacity].reshape(buffer_rows, row_width)

    sent_query, sent_key, sent_value, sent_grad = (unbox(i) for i in range(4))
    gather_table = (
        routing_in[None, :] == jnp.arange(cluster_rows, dtype=jnp.int32)[:, None]
    ).astype(jnp.bfloat16)

    def gather_rows(rows_in):
        grouped = jnp.dot(gather_table, rows_in, preferred_element_type=jnp.float32).astype(
            jnp.bfloat16
        )
        return grouped.reshape(clusters_here, CLUSTER_SIZE, head_count, HEAD_DIM)

    def scatter_rows(grouped):
        flat_rows = grouped.reshape(cluster_rows, row_width)
        spread = lax.dot_general(
            gather_table, flat_rows, (((0,), (0,)), ((), ())), preferred_element_type=jnp.float32
        )
        return spread.astype(jnp.bfloat16)

    query_rows = gather_rows(sent_query)
    key_rows = gather_rows(sent_key)
    value_rows = gather_rows(sent_value)
    attention, attn_low, attended = attend(query_rows, key_rows, value_rows, score_scale)
    sums = jnp.pad(key_centroids(key_rows), ((0, 8 - clusters_here), (0, 0)))
    grad_rows = gather_rows(sent_grad)
    grad_query, grad_key, grad_value = backprop(
        query_rows, key_rows, value_rows, grad_rows, attention, attn_low, score_scale
    )
    boxes = jnp.concatenate(
        [
            scatter_rows(a).reshape(shards, capacity, row_width)
            for a in (attended, grad_query, grad_key, grad_value)
        ],
        axis=1,
    ).reshape(shards, 2, 2 * capacity, row_width)
    rows_back, means = collect(boxes, held_slots, sums)
    back = rows_back.reshape(4, tok_rows, row_width)
    return (back[0], back[1], back[2], back[3], means[:clusters_here])


def solution(mesh):
    placed = (
        P("seq", "head"),
        P("seq", "head"),
        P("seq", "head"),
        P("seq", "head"),
        P("seq", None),
        P("seq", None),
    )
    return jax.shard_map(
        local,
        mesh=mesh,
        in_specs=placed,
        out_specs=(
            P("seq", "head"),
            P("seq", "head"),
            P("seq", "head"),
            P("seq", "head"),
            P("seq", None),
        ),
        check_vma=False,
    )
```

```python
import functools
import math

import jax
import jax.numpy as jnp
from jax import lax
from jax.experimental import pallas as pl
from jax.experimental.pallas import tpu as pltpu
from jax.sharding import PartitionSpec as P

HEAD_DIM = 128
CLUSTER_SIZE = 256
RING = 16
HEADS = 4
PEERS = 8
MESH = pl.DeviceIdType.MESH
NEAR_FIRST = (0, 1, -1, 2, -2, 3, -3, 4)
FAR_FIRST = (4, 3, -3, 2, -2, 1, -1, 0)


def place():
    me = lax.axis_index("seq")
    head = lax.axis_index("head")
    return (me, head, me // (2 * RING), lax.rem(me // 2, RING), lax.rem(me, 2))


def device_at(column, height, core):
    return (column * RING + height) * 2 + core


def around(value, size):
    return lax.rem(value + size, size)


def signal(barrier, seq, head):
    pl.semaphore_signal(barrier, inc=1, device_id=(seq, head), device_id_type=MESH)


def remote(source, target, send_sem, recv_sem, seq, head):
    return pltpu.make_async_remote_copy(
        src_ref=source,
        dst_ref=target,
        send_sem=send_sem,
        recv_sem=recv_sem,
        device_id=(seq, head),
        device_id_type=MESH,
    )


def loop(first, last, body):
    def step(index, carry):
        body(index)
        return carry

    lax.fori_loop(first, last, step, 0)


def hit_table(first_row, second_row, head):
    shape = (512, 512)
    row = lax.broadcasted_iota(jnp.int32, shape, 0)
    lane = lax.broadcasted_iota(jnp.int32, shape, 1)
    peer = row // 64
    device = ((peer // 2) * HEADS + head) * 2 + peer % 2
    wanted = (device * 4 + row // 16 % 4) * 8 + row % 8
    half = shape[1] // 2
    copies = [
        jnp.concatenate([first_row[:, c * half : (c + 1) * half], second_row[:, c * half : (c + 1) * half]], axis=1)
        for c in range(2)
    ]
    hit = (copies[0] == wanted) | (copies[1] == wanted)
    same = row // 8 % 2 == lane // half
    return jnp.where(hit & same, 1.0, 0.0).astype(jnp.bfloat16)


def spread_kernel(
    shards, rows_ref, slots_ref, lines_ref, boxes_ref, held_slots_ref, held_lines_ref,
    full, packed, slot_send, slot_recv, line_send, line_recv,
    z_send, z_recv, y_send, y_recv, x_send, x_recv, own_sem,
):
    me, head, column, height, core = place()
    mine = column * 2 + core
    here = lax.rem(height, HEADS) == head
    barrier = pltpu.get_barrier_semaphore()
    loop(1, shards, lambda step: signal(barrier, lax.rem(me + step, shards), head))
    for step in (1, HEADS - 1):
        signal(barrier, me, lax.rem(head + step, HEADS))

    def greet_source(source):
        @pl.when(jnp.logical_not(here & (source == height)))
        def _():
            signal(barrier, device_at(column, source, core), lax.rem(height, HEADS))

    loop(0, RING, greet_source)
    held_slots_ref[height] = slots_ref[...]
    held_lines_ref[me] = lines_ref[mine]
    pl.semaphore_wait(barrier, shards - 1 + 2 + RING - jnp.where(here, 1, 0))

    def send_slots(step):
        peer = device_at(column, lax.rem(height + step, RING), core)
        remote(slots_ref, held_slots_ref.at[height], slot_send, slot_recv, peer, head).start()

    loop(1, RING, send_slots)

    def send_quarter(index):
        turn = lax.rem(index // 4, 4)
        quad = lax.rem(height // 4 + jnp.where(turn == 2, 3, jnp.where(turn == 3, 2, turn)), 4)
        quarter = lax.rem(head + index, HEADS)
        plane = 4 * quad + head
        source = rows_ref.at[quad, pl.ds(pl.multiple_of(quarter * 64, 64), 64)]
        target = full.at[height, quarter]
        stays = (plane == height) & (quarter == head)

        @pl.when(stays)
        def _():
            pltpu.make_async_copy(source, target, z_recv.at[height]).start()

        @pl.when(jnp.logical_not(stays))
        def _():
            remote(
                source, target, z_send, z_recv.at[height],
                device_at(column, plane, core), quarter,
            ).start()

    loop(0, RING, send_quarter)

    def send_line(step):
        peer = lax.rem(me + step, shards)
        peer_column = peer // (2 * RING) * 2 + lax.rem(peer, 2)
        remote(
            lines_ref.at[peer_column], held_lines_ref.at[me], line_send, line_recv, peer, head
        ).start()

    loop(1, shards, send_line)

    def y_copy(source, quarter, step, kind):
        part = full.at[source, around(quarter, HEADS)]
        return remote(
            part, part, y_send, y_recv.at[kind, source], me, around(head + step, HEADS)
        )

    def pair_at(turn):
        return lax.rem(height // 2 + NEAR_FIRST[turn] + 8, 8)

    def share(turn):
        for side in range(2):
            source = pair_at(turn) * 2 + side
            part = full.at[source, head]
            remote(part, part, z_send, z_recv.at[source], me, head).wait_recv()
            y_copy(source, head, 1, 0).start()
            y_copy(source, head, -1, 1).start()

    def relay(turn):
        for side in range(2):
            source = pair_at(turn) * 2 + side
            if side == 0:
                y_copy(source, head - 1, 1, 0).wait_recv()
                y_copy(source, head - 1, 1, 2).start()
                y_copy(source, head + 1, -1, 1).wait_recv()
            else:
                y_copy(source, head + 1, -1, 1).wait_recv()
                y_copy(source, head + 1, -1, 2).start()
                y_copy(source, head - 1, 1, 0).wait_recv()

    def deliver(turn):
        pair = pair_at(turn)
        for side in range(2):
            y_copy(pair * 2 + side, head + 2, 1, 2).wait_recv()
        table = hit_table(held_slots_ref[pair * 2], held_slots_ref[pair * 2 + 1], head)
        tokens = full[pl.ds(pair * 2, 2)].reshape(512, 512)
        result = jnp.dot(table, tokens, preferred_element_type=jnp.float32)
        packed[turn] = result.astype(jnp.bfloat16).reshape(PEERS, 64, 512)
        target = boxes_ref.at[mine * 8 + pair]
        pltpu.make_async_copy(packed.at[turn, mine], target, own_sem.at[turn]).start()

        def send(step):
            peer = lax.rem(mine + step, PEERS)
            remote(
                packed.at[turn, peer], target, x_send, x_recv,
                device_at(peer // 2, height, lax.rem(peer, 2)), head,
            ).start()

        loop(1, PEERS, send)

    other = lax.rem(head + 1, HEADS)
    for turn in range(10):
        if turn < 8:
            share(turn)
        if 1 <= turn < 9:
            relay(turn - 1)
        if turn == 2:
            lot = held_slots_ref.at[pl.ds(0, RING - 1)]
            remote(lot, lot, slot_send, slot_recv, me, other).wait()
        if turn >= 2:
            deliver(turn - 2)
    for turn in range(8):
        pltpu.make_async_copy(
            packed.at[turn, mine], boxes_ref.at[mine * 8 + turn], own_sem.at[turn]
        ).wait()
    lot = boxes_ref.at[pl.ds(0, 56)]
    remote(lot, lot, x_send, x_recv, me, other).wait()
    lot = held_lines_ref.at[pl.ds(0, shards - 1)]
    remote(lot, lot, line_send, line_recv, me, other).wait()
    lot = full.at[pl.ds(0, 12)]
    remote(lot, lot, y_send, y_recv.at[0, 0], me, other).wait_send()

    def sent_quarter(index):
        part = full.at[0, 0]
        remote(part, part, z_send, z_recv.at[0], me, other).wait_send()

    loop(0, RING - jnp.where(here, 1, 0), sent_quarter)


def spread(rows, slots, lines, shards):
    vmem = pl.BlockSpec(memory_space=pltpu.VMEM)
    dma = pltpu.SemaphoreType.DMA
    return pl.pallas_call(
        functools.partial(spread_kernel, shards),
        out_shape=(
            jax.ShapeDtypeStruct((64, 64, 512), jnp.bfloat16),
            jax.ShapeDtypeStruct((RING,) + slots.shape, jnp.int32),
            jax.ShapeDtypeStruct((shards,) + lines.shape[1:], jnp.int32),
        ),
        in_specs=[vmem] * 3,
        out_specs=(vmem,) * 3,
        scratch_shapes=[
            pltpu.VMEM((RING, 4, 64, 512), jnp.bfloat16),
            pltpu.VMEM((8, PEERS, 64, 512), jnp.bfloat16),
            dma, dma, dma, dma,
            dma, dma((RING,)), dma, dma((3, RING)), dma, dma, dma((8,)),
        ],
        compiler_params=pltpu.CompilerParams(
            collective_id=0, has_side_effects=True, vmem_limit_bytes=48 * 2**20
        ),
    )(rows, slots, lines)


def collect_kernel(
    boxes_ref, held_slots_ref, sums_ref, rows_ref, means_ref,
    held, part, far, near, done, sums, x_send, x_recv, own_sem,
    y_send, far_recv, near_recv, z_send, z_recv, sum_send, sum_recv,
):
    me, head, column, height, core = place()
    mine = column * 2 + core
    here = lax.rem(height, HEADS) == head
    owner = (height // 4 == head) & (lax.rem(height // 2, 2) == core)
    barrier = pltpu.get_barrier_semaphore()

    def greet_peer(step):
        peer = lax.rem(mine + step, PEERS)
        signal(barrier, device_at(peer // 2, height, lax.rem(peer, 2)), head)

    loop(1, PEERS, greet_peer)
    for step in (1, HEADS - 1):
        signal(barrier, me, lax.rem(head + step, HEADS))

    def greet_relay(index):
        plane = index // 4 * 4 + head
        quarter = lax.rem(index, 4)

        @pl.when(jnp.logical_not((plane == height) & (quarter == head)))
        def _():
            signal(barrier, device_at(column, plane, core), quarter)

    loop(0, RING, greet_relay)

    def greet_summer(plane):
        @pl.when(jnp.logical_not(owner & (plane == height)))
        def _():
            signal(barrier, device_at(column, plane, lax.rem(height // 2, 2)), height // 4)

    loop(0, RING, greet_summer)
    pl.semaphore_wait(
        barrier, PEERS - 1 + 2 + 2 * RING - jnp.where(here, 1, 0) - jnp.where(owner, 1, 0)
    )

    def pair_at(turn):
        return lax.rem(height // 2 + FAR_FIRST[turn] + 8, 8)

    for turn in range(8):
        pair = pair_at(turn)
        pltpu.make_async_copy(
            boxes_ref.at[mine * 8 + pair], held.at[pair, mine], own_sem.at[turn]
        ).start()

        def send_box(step):
            peer = lax.rem(mine + step, PEERS)
            remote(
                boxes_ref.at[peer * 8 + pair], held.at[pair, mine], x_send, x_recv.at[pair],
                device_at(peer // 2, height, lax.rem(peer, 2)), head,
            ).start()

        loop(1, PEERS, send_box)

    def send_sum(index):
        group = index // 4
        there = lax.rem(head + index, HEADS)
        peer = device_at(column, (head * 2 + core) * 2 + group // 2, lax.rem(group, 2))
        stays = (peer == me) & (there == head)

        @pl.when(stays)
        def _():
            pltpu.make_async_copy(sums_ref.at[group], sums.at[height], sum_recv).start()

        @pl.when(jnp.logical_not(stays))
        def _():
            remote(
                sums_ref.at[group], sums.at[height], sum_send, sum_recv, peer, there
            ).start()

    loop(0, RING, send_sum)

    def up(source, quarter, target, recv):
        return remote(
            part.at[source, around(quarter, HEADS)], target, y_send, recv, me,
            around(head + 1, HEADS),
        )

    def down(source, quarter, target, recv):
        return remote(
            part.at[source, around(quarter, HEADS)], target, y_send, recv, me,
            around(head - 1, HEADS),
        )

    def unpack(turn):
        pair = pair_at(turn)
        pltpu.make_async_copy(
            boxes_ref.at[mine * 8 + pair], held.at[pair, mine], own_sem.at[turn]
        ).wait()
        lot = held.at[pair, pl.ds(0, PEERS - 1)]
        remote(lot, lot, x_send, x_recv.at[pair], me, around(head + 1, HEADS)).wait_recv()
        table = hit_table(held_slots_ref[pair * 2], held_slots_ref[pair * 2 + 1], head)
        result = lax.dot_general(
            table, held[pair].reshape(512, 512), (((0,), (0,)), ((), ())),
            preferred_element_type=jnp.float32,
        )
        part[pl.ds(pair * 2, 2)] = result.astype(jnp.bfloat16).reshape(2, 4, 64, 512)
        even, odd = (pair * 2, pair * 2 + 1)
        up(even, head + 2, far.at[even], far_recv.at[even]).start()
        down(even, head - 1, near.at[1, even], near_recv.at[1, even]).start()
        down(odd, head + 2, far.at[odd], far_recv.at[odd]).start()
        up(odd, head + 1, near.at[0, odd], near_recv.at[0, odd]).start()

    def join(turn):
        even = pair_at(turn) * 2
        for source, step in ((even, 1), (even + 1, -1)):
            spot = around(head + step, HEADS)
            up(source, head + step, far.at[source], far_recv.at[source]).wait_recv()
            total = part[source, spot].astype(jnp.float32) + far[source].astype(jnp.float32)
            part[source, spot] = total.astype(jnp.bfloat16)
            if step == 1:
                up(source, head + 1, near.at[0, source], near_recv.at[0, source]).start()
            else:
                down(source, head - 1, near.at[1, source], near_recv.at[1, source]).start()

    def finish(turn):
        for side in range(2):
            source = pair_at(turn) * 2 + side
            total = part[source, head].astype(jnp.float32)
            for way in range(2):
                up(source, head, near.at[way, source], near_recv.at[way, source]).wait_recv()
                total += near[way, source].astype(jnp.float32)
            done[source] = total.astype(jnp.bfloat16)
            target = rows_ref.at[height // 4, head]
            stays = here & (source == height)

            @pl.when(stays)
            def _():
                pltpu.make_async_copy(done.at[source], target, z_recv).start()

            @pl.when(jnp.logical_not(stays))
            def _():
                remote(
                    done.at[source], target, z_send, z_recv,
                    device_at(column, source, core), lax.rem(height, HEADS),
                ).start()

    for turn in range(10):
        if turn < 8:
            unpack(turn)
        if 1 <= turn < 9:
            join(turn - 1)
        if turn >= 2:
            finish(turn - 2)
    other = around(head + 1, HEADS)
    remote(sums, sums, sum_send, sum_recv, me, other).wait_recv()
    grand = sums[0]
    for plane in range(1, RING):
        grand += sums[plane]
    means_ref[...] = grand * lax.rsqrt(jnp.mean(grand * grand, axis=1, keepdims=True) + 1e-06)
    lot = boxes_ref.at[pl.ds(0, 56)]
    remote(lot, lot, x_send, x_recv.at[0], me, other).wait_send()
    lot = part.at[pl.ds(0, 12)]
    remote(lot, lot, y_send, far_recv.at[0], me, other).wait_send()

    def sent_sum(index):
        remote(sums.at[0], sums.at[0], sum_send, sum_recv, me, other).wait_send()

    loop(0, RING - jnp.where(owner, 1, 0), sent_sum)

    def sent_rows(index):
        remote(done.at[0], done.at[0], z_send, z_recv, me, other).wait_send()

    loop(0, RING - jnp.where(here, 1, 0), sent_rows)
    remote(rows_ref, rows_ref, z_send, z_recv, me, other).wait_recv()


def collect(boxes, held_slots, sums):
    vmem = pl.BlockSpec(memory_space=pltpu.VMEM)
    dma = pltpu.SemaphoreType.DMA
    return pl.pallas_call(
        collect_kernel,
        out_shape=(
            jax.ShapeDtypeStruct((4, 4, 64, 512), jnp.bfloat16),
            jax.ShapeDtypeStruct(sums.shape[1:], jnp.float32),
        ),
        in_specs=[vmem] * 3,
        out_specs=(vmem,) * 2,
        scratch_shapes=[
            pltpu.VMEM((8, PEERS, 64, 512), jnp.bfloat16),
            pltpu.VMEM((RING, 4, 64, 512), jnp.bfloat16),
            pltpu.VMEM((RING, 64, 512), jnp.bfloat16),
            pltpu.VMEM((2, RING, 64, 512), jnp.bfloat16),
            pltpu.VMEM((RING, 64, 512), jnp.bfloat16),
            pltpu.VMEM((RING,) + sums.shape[1:], jnp.float32),
            dma, dma((8,)), dma((8,)),
            dma, dma((RING,)), dma((2, RING)), dma, dma, dma, dma,
        ],
        compiler_params=pltpu.CompilerParams(
            collective_id=1, has_side_effects=True, vmem_limit_bytes=48 * 2**20
        ),
    )(boxes, held_slots, sums)


def attend(query_rows, key_rows, value_rows, score_scale):
    scores = (
        jnp.einsum("cqhd,ckhd->chqk", query_rows, key_rows, preferred_element_type=jnp.float32)
        * score_scale
    )
    slot_order = jnp.arange(query_rows.shape[1], dtype=jnp.int32)
    allowed = slot_order[None, :] <= slot_order[:, None]
    scores = jnp.where(allowed, scores, jnp.float32(-1e30))
    row_max = jnp.max(scores, axis=3, keepdims=True)
    weights = jnp.exp(scores - row_max)
    attention = weights / jnp.sum(weights, axis=3, keepdims=True)
    attn_low = attention.astype(jnp.bfloat16)
    attended = jnp.einsum(
        "chqk,ckhd->cqhd", attn_low, value_rows, preferred_element_type=jnp.float32
    )
    return (attention, attn_low, attended.astype(jnp.bfloat16))


def backprop(query_rows, key_rows, value_rows, grad_rows, attention, attn_low, score_scale):
    prob_grad = jnp.einsum(
        "cqhd,ckhd->chqk", grad_rows, value_rows, preferred_element_type=jnp.float32
    )
    row_dot = jnp.sum(attention * prob_grad, axis=3, keepdims=True)
    grad_score = (attention * (prob_grad - row_dot) * score_scale).astype(jnp.bfloat16)
    grad_query = jnp.einsum(
        "chqk,ckhd->cqhd", grad_score, key_rows, preferred_element_type=jnp.float32
    )
    grad_key = jnp.einsum(
        "chqk,cqhd->ckhd", grad_score, query_rows, preferred_element_type=jnp.float32
    )
    grad_value = jnp.einsum(
        "chqk,cqhd->ckhd", attn_low, grad_rows, preferred_element_type=jnp.float32
    )
    return (
        grad_query.astype(jnp.bfloat16),
        grad_key.astype(jnp.bfloat16),
        grad_value.astype(jnp.bfloat16),
    )


def key_centroids(key_rows):
    key_float = key_rows.astype(jnp.float32)
    normed = key_float * lax.rsqrt(jnp.mean(key_float * key_float, axis=3, keepdims=True) + 1e-06)
    return jnp.sum(normed, axis=(1, 2))


def local(queries, keys, values, out_grad, cluster_ids, slots):
    tok_rows = queries.shape[0]
    shards = lax.axis_size("seq")
    score_scale = 1.0 / math.sqrt(HEAD_DIM)
    groups = (cluster_ids // 2).reshape(-1)
    group_hits = (groups[:, None] == jnp.arange(shards, dtype=jnp.int32)[None, :]).astype(jnp.int32)
    earlier = jnp.cumsum(group_hits, axis=0) - group_hits
    buffer_slot = groups * 8 + jnp.sum(earlier * group_hits, axis=1)
    targets = (cluster_ids % 2 * CLUSTER_SIZE + slots).reshape(-1)
    routing = jnp.full((shards * 8,), -1, jnp.int32).at[buffer_slot].set(targets)
    lines = lax.dynamic_index_in_dim(
        routing.reshape(4, HEADS, 2, 32), lax.axis_index("head"), axis=1, keepdims=False
    )
    lines = jnp.pad(lines.reshape(PEERS, 1, 32), ((0, 0), (0, 0), (0, 96)))
    slot_row = buffer_slot.reshape(tok_rows, 2).T.reshape(1, 2 * tok_rows)

    def by_head(rows_in):
        return rows_in.reshape(tok_rows, HEADS, HEAD_DIM).transpose(1, 0, 2)

    sent = jnp.concatenate([by_head(a) for a in (queries, keys, values, out_grad)], axis=2)
    arrived, held_slots, held_lines = spread(sent, slot_row, lines, shards)
    routing_in = (
        held_lines[:, 0, :32]
        .reshape(4, 8, 2, 2, 4, 8)
        .transpose(4, 0, 3, 1, 2, 5)
        .reshape(4, 1024)
    )
    gather_table = (
        routing_in[:, None, :] == jnp.arange(512, dtype=jnp.int32)[None, :, None]
    ).astype(jnp.bfloat16)
    arrived = arrived.reshape(64, 4, 16, 512).transpose(1, 0, 2, 3).reshape(4, 1024, 512)
    grouped = jnp.einsum(
        "grs,gsd->grd", gather_table, arrived, preferred_element_type=jnp.float32
    ).astype(jnp.bfloat16)
    query_rows, key_rows, value_rows, grad_rows = (
        grouped[:, :, i * HEAD_DIM : (i + 1) * HEAD_DIM].reshape(8, CLUSTER_SIZE, 1, HEAD_DIM)
        for i in range(4)
    )
    attention, attn_low, attended = attend(query_rows, key_rows, value_rows, score_scale)
    sums = jnp.pad(key_centroids(key_rows).reshape(4, 2, HEAD_DIM), ((0, 0), (0, 6), (0, 0)))
    grads = backprop(
        query_rows, key_rows, value_rows, grad_rows, attention, attn_low, score_scale
    )
    results = jnp.concatenate([a.reshape(4, 512, HEAD_DIM) for a in (attended,) + grads], axis=2)
    boxes = jnp.einsum(
        "grs,grd->gsd", gather_table, results, preferred_element_type=jnp.float32
    ).astype(jnp.bfloat16)
    boxes = boxes.reshape(4, 64, 16, 512).transpose(1, 0, 2, 3).reshape(64, 64, 512)
    rows_back, means = collect(boxes, held_slots, sums)
    back = rows_back.reshape(HEADS, tok_rows, 4, HEAD_DIM)
    outs = tuple(
        back[:, :, i].transpose(1, 0, 2).reshape(tok_rows, HEADS * HEAD_DIM) for i in range(4)
    )
    return outs + (means[:2],)


def solution(mesh):
    placed = (
        P("seq", "head"),
        P("seq", "head"),
        P("seq", "head"),
        P("seq", "head"),
        P("seq", None),
        P("seq", None),
    )
    return jax.shard_map(
        local,
        mesh=mesh,
        in_specs=placed,
        out_specs=(
            P("seq", "head"),
            P("seq", "head"),
            P("seq", "head"),
            P("seq", "head"),
            P("seq", None),
        ),
        check_vma=False,
    )
```

```python
import functools
import math

import jax
import jax.numpy as jnp
from jax import lax
from jax.experimental import pallas as pl
from jax.experimental.pallas import tpu as pltpu
from jax.sharding import PartitionSpec as P

HEAD_DIM = 128
CLUSTER_SIZE = 256
RING = 16
HEADS = 4
PEERS = 8
MESH = pl.DeviceIdType.MESH
OUTWARD = (0, 1, 4, -3, -2, 3, 2, -1)
RETURN = (4, 3, -2, -3, 2, 1, 0, -1)
AHEAD = 3


def place():
    me = lax.axis_index("seq")
    head = lax.axis_index("head")
    return (me, head, me // (2 * RING), lax.rem(me // 2, RING), lax.rem(me, 2))


def device_at(column, height, core):
    return (column * RING + height) * 2 + core


def around(value, size):
    return lax.rem(value + size, size)


def signal(barrier, seq, head):
    pl.semaphore_signal(barrier, inc=1, device_id=(seq, head), device_id_type=MESH)


def remote(source, target, send_sem, recv_sem, seq, head):
    return pltpu.make_async_remote_copy(
        src_ref=source,
        dst_ref=target,
        send_sem=send_sem,
        recv_sem=recv_sem,
        device_id=(seq, head),
        device_id_type=MESH,
    )


def loop(first, last, body):
    def step(index, carry):
        body(index)
        return carry

    lax.fori_loop(first, last, step, 0)


def hit_table(notes_ref, pair, head):
    shape = (512, 512)
    row = lax.broadcasted_iota(jnp.int32, shape, 0)
    lane = lax.broadcasted_iota(jnp.int32, shape, 1)
    peer = row // 64
    device = ((peer // 2) * HEADS + head) * 2 + peer % 2
    wanted = (device * 4 + row // 16 % 4) * 8 + row % 8
    copies = [
        jnp.concatenate(
            [notes_ref[pair * 2 + side, 2 * c + part] for side in range(2) for part in range(2)],
            axis=1,
        )
        for c in range(2)
    ]
    hit = (copies[0] == wanted) | (copies[1] == wanted)
    same = row // 8 % 2 == lane // 256
    return jnp.where(hit & same, 1.0, 0.0).astype(jnp.bfloat16)


def spread_kernel(
    rows_ref, notes_ref, boxes_ref, held_notes_ref, lines_ref,
    spread_rows, full, packed, note_send, note_recv, line_send, line_recv, line_own,
    first_send, first_recv, stay_sem, z_send, z_recv, y_send, y_recv, x_send, x_recv, own_sem,
):
    me, head, column, height, core = place()
    mine = column * 2 + core
    barrier = pltpu.get_barrier_semaphore()

    def greet_ring(step):
        signal(barrier, device_at(column, lax.rem(height + step, RING), core), head)

    loop(1, RING, greet_ring)

    def greet_peer(step):
        peer = lax.rem(mine + step, PEERS)
        signal(barrier, device_at(peer // 2, height, lax.rem(peer, 2)), head)

    loop(1, PEERS, greet_peer)
    for step in range(1, HEADS):
        signal(barrier, me, lax.rem(head + step, HEADS))
    other = lax.rem(head + 1, HEADS)
    held_notes_ref[height] = notes_ref[...]
    pl.semaphore_wait(barrier, RING - 1 + PEERS - 1 + HEADS - 1)

    def send_notes(step):
        peer = device_at(column, lax.rem(height + step, RING), core)
        remote(notes_ref, held_notes_ref.at[height], note_send, note_recv, peer, head).start()

    def first_copy(quad, step):
        there = lax.rem(head + step, HEADS)
        return remote(
            rows_ref.at[quad, pl.ds(pl.multiple_of(there * 64, 64), 64)],
            spread_rows.at[head, quad],
            first_send,
            first_recv.at[head, quad],
            me,
            there,
        )

    for step in (0, 3, 2, 1):
        quad = lax.rem(height // 4 + step, 4)
        for way in range(1, HEADS):
            first_copy(quad, way).start()
        own = rows_ref.at[quad, pl.ds(pl.multiple_of(head * 64, 64), 64)]
        pltpu.make_async_copy(own, spread_rows.at[head, quad], first_recv.at[head, quad]).start()

    def stay_copy():
        return pltpu.make_async_copy(
            spread_rows.at[lax.rem(height, HEADS), height // 4], full.at[height, head], stay_sem
        )

    def send_quarters(turn):
        there = lax.rem(height // 2 - OUTWARD[turn] + 8, 8)

        def send_quarter(side):
            plane = there * 2 + side
            row_head, quad = (lax.rem(plane, HEADS), plane // 4)
            source = spread_rows.at[row_head, quad]
            pltpu.make_async_copy(source, source, first_recv.at[row_head, quad]).wait()

            @pl.when(plane == height)
            def _():
                stay_copy().start()

            @pl.when(plane != height)
            def _():
                remote(
                    source, full.at[height, head], z_send, z_recv.at[height],
                    device_at(column, plane, core), head,
                ).start()

        loop(0, 2, send_quarter)

    for turn in range(AHEAD):
        send_quarters(turn)
    loop(1, RING, send_notes)

    def y_copy(source, quarter, step, kind):
        part = full.at[source, around(quarter, HEADS)]
        return remote(
            part, part, y_send, y_recv.at[kind, source], me, around(head + step, HEADS)
        )

    def pair_at(turn):
        return lax.rem(height // 2 + OUTWARD[turn] + 8, 8)

    def share(turn):
        for side in range(2):
            source = pair_at(turn) * 2 + side
            part = full.at[source, head]

            @pl.when(source == height)
            def _():
                stay_copy().wait()

            @pl.when(source != height)
            def _():
                remote(part, part, z_send, z_recv.at[source], me, other).wait_recv()

            y_copy(source, head, 1, 0).start()
            y_copy(source, head, -1, 1).start()

    def relay(turn):
        for side in range(2):
            source = pair_at(turn) * 2 + side
            if side == 0:
                y_copy(source, head - 1, 1, 0).wait_recv()
                y_copy(source, head - 1, 1, 2).start()
                y_copy(source, head + 1, -1, 1).wait_recv()
            else:
                y_copy(source, head + 1, -1, 1).wait_recv()
                y_copy(source, head + 1, -1, 2).start()
                y_copy(source, head - 1, 1, 0).wait_recv()

    def deliver(turn):
        pair = pair_at(turn)
        for side in range(2):
            y_copy(pair * 2 + side, head + 2, 1, 2).wait_recv()
        table = hit_table(held_notes_ref, pair, head)
        tokens = full[pl.ds(pair * 2, 2)].reshape(512, 512)
        result = jnp.dot(table, tokens, preferred_element_type=jnp.float32)
        packed[turn] = result.astype(jnp.bfloat16).reshape(PEERS, 4, 16, 512)
        target = boxes_ref.at[mine * 8 + pair]
        pltpu.make_async_copy(packed.at[turn, mine], target, own_sem.at[turn]).start()

        def send(step):
            peer = lax.rem(mine + step, PEERS)
            remote(
                packed.at[turn, peer], target, x_send, x_recv,
                device_at(peer // 2, height, lax.rem(peer, 2)), head,
            ).start()

        loop(1, PEERS, send)

    def send_lines(step):
        peer = lax.rem(mine + step, PEERS)
        remote(
            held_notes_ref.at[pl.ds(0, RING), 4 + peer], lines_ref.at[mine], line_send, line_recv,
            device_at(peer // 2, height, lax.rem(peer, 2)), head,
        ).start()

    own_lines = pltpu.make_async_copy(
        held_notes_ref.at[pl.ds(0, RING), 4 + mine], lines_ref.at[mine], line_own
    )
    for turn in range(10):
        if turn < 8:
            share(turn)
        if turn + AHEAD < 8:
            send_quarters(turn + AHEAD)
        if 1 <= turn < 9:
            relay(turn - 1)
        if turn == 2:
            lot = held_notes_ref.at[pl.ds(0, RING - 1)]
            remote(lot, lot, note_send, note_recv, me, other).wait()
            own_lines.start()
            loop(1, PEERS, send_lines)
        if turn >= 2:
            deliver(turn - 2)
    for turn in range(8):
        pltpu.make_async_copy(
            packed.at[turn, mine], boxes_ref.at[mine * 8 + turn], own_sem.at[turn]
        ).wait()
    lot = boxes_ref.at[pl.ds(0, 56)]
    remote(lot, lot, x_send, x_recv, me, other).wait()
    own_lines.wait()
    lot = lines_ref.at[pl.ds(0, PEERS - 1)]
    remote(lot, lot, line_send, line_recv, me, other).wait()
    lot = full.at[pl.ds(0, 12)]
    remote(lot, lot, y_send, y_recv.at[0, 0], me, other).wait_send()

    def sent_quarter(index):
        part = full.at[0, 0]
        remote(part, part, z_send, z_recv.at[0], me, other).wait_send()

    loop(0, RING - 1, sent_quarter)
    lot = spread_rows.at[pl.ds(0, HEADS - 1)]
    remote(lot, lot, first_send, first_recv.at[0, 0], me, other).wait_send()


def spread(rows, notes):
    vmem = pl.BlockSpec(memory_space=pltpu.VMEM)
    dma = pltpu.SemaphoreType.DMA
    return pl.pallas_call(
        spread_kernel,
        out_shape=(
            jax.ShapeDtypeStruct((64, 4, 16, 512), jnp.bfloat16),
            jax.ShapeDtypeStruct((RING,) + notes.shape, jnp.int32),
            jax.ShapeDtypeStruct((PEERS, RING) + notes.shape[1:], jnp.int32),
        ),
        in_specs=[vmem] * 2,
        out_specs=(vmem,) * 3,
        scratch_shapes=[
            pltpu.VMEM((HEADS, 4, 64, 512), jnp.bfloat16),
            pltpu.VMEM((RING, 4, 64, 512), jnp.bfloat16),
            pltpu.VMEM((8, PEERS, 4, 16, 512), jnp.bfloat16),
            dma, dma, dma, dma, dma,
            dma, dma((HEADS, 4)), dma,
            dma, dma((RING,)), dma, dma((3, RING)), dma, dma, dma((8,)),
        ],
        compiler_params=pltpu.CompilerParams(
            collective_id=0, has_side_effects=True, vmem_limit_bytes=48 * 2**20
        ),
    )(rows, notes)


def product(left, right, left_dim, right_dim):
    return lax.dot_general(
        left, right, (((left_dim,), (right_dim,)), ((), ())), preferred_element_type=jnp.float32
    )


def attend_kernel(lines_ref, rows_ref, boxes_ref, sums_ref, results):
    scale = 1.0 / math.sqrt(HEAD_DIM)
    shape = (512, 1024)
    row = lax.broadcasted_iota(jnp.int32, shape, 0)
    table = jnp.where(lines_ref[0] == row, 1.0, 0.0).astype(jnp.bfloat16)
    grouped = product(table, rows_ref[...].reshape(1024, 512), 1, 0).astype(jnp.bfloat16)
    size = (CLUSTER_SIZE, CLUSTER_SIZE)
    allowed = lax.broadcasted_iota(jnp.int32, size, 1) <= lax.broadcasted_iota(jnp.int32, size, 0)
    sums_ref[...] = jnp.zeros_like(sums_ref)
    for cluster in range(2):
        first = cluster * CLUSTER_SIZE
        query, key, value, grad = (
            grouped[first : first + CLUSTER_SIZE, i * HEAD_DIM : (i + 1) * HEAD_DIM]
            for i in range(4)
        )
        scores = jnp.where(allowed, product(query, key, 1, 1) * scale, jnp.float32(-1e30))
        weights = jnp.exp(scores - jnp.max(scores, axis=1, keepdims=True))
        attention = weights / jnp.sum(weights, axis=1, keepdims=True)
        attn_low = attention.astype(jnp.bfloat16)
        prob_grad = product(grad, value, 1, 1)
        row_dot = jnp.sum(attention * prob_grad, axis=1, keepdims=True)
        grad_score = (attention * (prob_grad - row_dot) * scale).astype(jnp.bfloat16)
        outs = (
            product(attn_low, value, 1, 0),
            product(grad_score, key, 1, 0),
            product(grad_score, query, 0, 0),
            product(attn_low, grad, 0, 0),
        )
        for i, out in enumerate(outs):
            results[first : first + CLUSTER_SIZE, i * HEAD_DIM : (i + 1) * HEAD_DIM] = out.astype(
                jnp.bfloat16
            )
        key_float = key.astype(jnp.float32)
        normed = key_float * lax.rsqrt(
            jnp.mean(key_float * key_float, axis=1, keepdims=True) + 1e-06
        )
        sums_ref[0, cluster : cluster + 1] = jnp.sum(normed, axis=0, keepdims=True)
    boxes = product(table, results[...], 0, 0)
    boxes_ref[...] = boxes.astype(jnp.bfloat16).reshape(64, 1, 16, 512)


def attend_groups(lines, boxes):
    box_spec = pl.BlockSpec((64, 1, 16, 512), lambda group: (0, group, 0, 0))
    return pl.pallas_call(
        attend_kernel,
        grid=(4,),
        out_shape=(
            jax.ShapeDtypeStruct(boxes.shape, jnp.bfloat16),
            jax.ShapeDtypeStruct((4, 8, HEAD_DIM), jnp.float32),
        ),
        in_specs=[pl.BlockSpec((1, 1, 1024), lambda group: (group, 0, 0)), box_spec],
        out_specs=(box_spec, pl.BlockSpec((1, 8, HEAD_DIM), lambda group: (group, 0, 0))),
        scratch_shapes=[pltpu.VMEM((512, 512), jnp.bfloat16)],
        compiler_params=pltpu.CompilerParams(vmem_limit_bytes=48 * 2**20),
    )(lines, boxes)


def collect_kernel(
    boxes_ref, held_notes_ref, sums_ref, rows_ref, means_ref,
    held, part, far, near, done, sums, x_send, x_recv, own_sem,
    y_send, far_recv, near_recv, z_send, z_recv, sum_send, sum_recv,
):
    me, head, column, height, core = place()
    mine = column * 2 + core
    here = lax.rem(height, HEADS) == head
    owner = (height // 4 == head) & (lax.rem(height // 2, 2) == core)
    barrier = pltpu.get_barrier_semaphore()

    def greet_peer(step):
        peer = lax.rem(mine + step, PEERS)
        signal(barrier, device_at(peer // 2, height, lax.rem(peer, 2)), head)

    loop(1, PEERS, greet_peer)
    for step in (1, HEADS - 1):
        signal(barrier, me, lax.rem(head + step, HEADS))

    def greet_relay(index):
        plane = index // 4 * 4 + head
        quarter = lax.rem(index, 4)

        @pl.when(jnp.logical_not((plane == height) & (quarter == head)))
        def _():
            signal(barrier, device_at(column, plane, core), quarter)

    loop(0, RING, greet_relay)

    def greet_summer(plane):
        @pl.when(jnp.logical_not(owner & (plane == height)))
        def _():
            signal(barrier, device_at(column, plane, lax.rem(height // 2, 2)), height // 4)

    loop(0, RING, greet_summer)
    pl.semaphore_wait(
        barrier, PEERS - 1 + 2 + 2 * RING - jnp.where(here, 1, 0) - jnp.where(owner, 1, 0)
    )

    def pair_at(turn):
        return lax.rem(height // 2 + RETURN[turn] + 8, 8)

    def send_boxes(turn):
        pair = pair_at(turn)
        pltpu.make_async_copy(
            boxes_ref.at[mine * 8 + pair], held.at[pair, mine], own_sem.at[turn]
        ).start()

        def send_box(step):
            peer = lax.rem(mine + step, PEERS)
            remote(
                boxes_ref.at[peer * 8 + pair], held.at[pair, mine], x_send, x_recv.at[pair],
                device_at(peer // 2, height, lax.rem(peer, 2)), head,
            ).start()

        loop(1, PEERS, send_box)

    for turn in range(AHEAD):
        send_boxes(turn)

    def send_sum(index):
        group = index // 4
        there = lax.rem(head + index, HEADS)
        peer = device_at(column, (head * 2 + core) * 2 + group // 2, lax.rem(group, 2))
        stays = (peer == me) & (there == head)

        @pl.when(stays)
        def _():
            pltpu.make_async_copy(sums_ref.at[group], sums.at[height], sum_recv).start()

        @pl.when(jnp.logical_not(stays))
        def _():
            remote(
                sums_ref.at[group], sums.at[height], sum_send, sum_recv, peer, there
            ).start()

    loop(0, RING, send_sum)

    def up(source, quarter, target, recv):
        return remote(
            part.at[source, around(quarter, HEADS)], target, y_send, recv, me,
            around(head + 1, HEADS),
        )

    def down(source, quarter, target, recv):
        return remote(
            part.at[source, around(quarter, HEADS)], target, y_send, recv, me,
            around(head - 1, HEADS),
        )

    def unpack(turn):
        pair = pair_at(turn)
        pltpu.make_async_copy(
            boxes_ref.at[mine * 8 + pair], held.at[pair, mine], own_sem.at[turn]
        ).wait()
        lot = held.at[pair, pl.ds(0, PEERS - 1)]
        remote(lot, lot, x_send, x_recv.at[pair], me, around(head + 1, HEADS)).wait_recv()
        table = hit_table(held_notes_ref, pair, head)
        result = lax.dot_general(
            table, held[pair].reshape(512, 512), (((0,), (0,)), ((), ())),
            preferred_element_type=jnp.float32,
        )
        part[pl.ds(pair * 2, 2)] = result.astype(jnp.bfloat16).reshape(2, 4, 64, 512)
        even, odd = (pair * 2, pair * 2 + 1)
        up(even, head + 2, far.at[even], far_recv.at[even]).start()
        down(even, head - 1, near.at[1, even], near_recv.at[1, even]).start()
        down(odd, head + 2, far.at[odd], far_recv.at[odd]).start()
        up(odd, head + 1, near.at[0, odd], near_recv.at[0, odd]).start()

    def join(turn):
        even = pair_at(turn) * 2
        for source, step in ((even, 1), (even + 1, -1)):
            spot = around(head + step, HEADS)
            up(source, head + step, far.at[source], far_recv.at[source]).wait_recv()
            total = part[source, spot].astype(jnp.float32) + far[source].astype(jnp.float32)
            part[source, spot] = total.astype(jnp.bfloat16)
            if step == 1:
                up(source, head + 1, near.at[0, source], near_recv.at[0, source]).start()
            else:
                down(source, head - 1, near.at[1, source], near_recv.at[1, source]).start()

    def finish(turn):
        for side in range(2):
            source = pair_at(turn) * 2 + side
            total = part[source, head].astype(jnp.float32)
            for way in range(2):
                up(source, head, near.at[way, source], near_recv.at[way, source]).wait_recv()
                total += near[way, source].astype(jnp.float32)
            done[source] = total.astype(jnp.bfloat16)
            target = rows_ref.at[height // 4, head]
            stays = here & (source == height)

            @pl.when(stays)
            def _():
                pltpu.make_async_copy(done.at[source], target, z_recv).start()

            @pl.when(jnp.logical_not(stays))
            def _():
                remote(
                    done.at[source], target, z_send, z_recv,
                    device_at(column, source, core), lax.rem(height, HEADS),
                ).start()

    for turn in range(10):
        if turn < 8:
            unpack(turn)
        if turn + AHEAD < 8:
            send_boxes(turn + AHEAD)
        if 1 <= turn < 9:
            join(turn - 1)
        if turn >= 2:
            finish(turn - 2)
    other = around(head + 1, HEADS)
    remote(sums, sums, sum_send, sum_recv, me, other).wait_recv()
    grand = sums[0]
    for plane in range(1, RING):
        grand += sums[plane]
    means_ref[...] = grand * lax.rsqrt(jnp.mean(grand * grand, axis=1, keepdims=True) + 1e-06)
    lot = boxes_ref.at[pl.ds(0, 56)]
    remote(lot, lot, x_send, x_recv.at[0], me, other).wait_send()
    lot = part.at[pl.ds(0, 12)]
    remote(lot, lot, y_send, far_recv.at[0], me, other).wait_send()

    def sent_sum(index):
        remote(sums.at[0], sums.at[0], sum_send, sum_recv, me, other).wait_send()

    loop(0, RING - jnp.where(owner, 1, 0), sent_sum)

    def sent_rows(index):
        remote(done.at[0], done.at[0], z_send, z_recv, me, other).wait_send()

    loop(0, RING - jnp.where(here, 1, 0), sent_rows)
    remote(rows_ref, rows_ref, z_send, z_recv, me, other).wait_recv()


def collect(boxes, held_notes, sums):
    vmem = pl.BlockSpec(memory_space=pltpu.VMEM)
    dma = pltpu.SemaphoreType.DMA
    return pl.pallas_call(
        collect_kernel,
        out_shape=(
            jax.ShapeDtypeStruct((4, 4, 64, 512), jnp.bfloat16),
            jax.ShapeDtypeStruct(sums.shape[1:], jnp.float32),
        ),
        in_specs=[vmem] * 3,
        out_specs=(vmem,) * 2,
        scratch_shapes=[
            pltpu.VMEM((8, PEERS, 4, 16, 512), jnp.bfloat16),
            pltpu.VMEM((RING, 4, 64, 512), jnp.bfloat16),
            pltpu.VMEM((RING, 64, 512), jnp.bfloat16),
            pltpu.VMEM((2, RING, 64, 512), jnp.bfloat16),
            pltpu.VMEM((RING, 64, 512), jnp.bfloat16),
            pltpu.VMEM((RING,) + sums.shape[1:], jnp.float32),
            dma, dma((8,)), dma((8,)),
            dma, dma((RING,)), dma((2, RING)), dma, dma, dma, dma,
        ],
        compiler_params=pltpu.CompilerParams(
            collective_id=1, has_side_effects=True, vmem_limit_bytes=48 * 2**20
        ),
    )(boxes, held_notes, sums)


def local(queries, keys, values, out_grad, cluster_ids, slots):
    tok_rows = queries.shape[0]
    shards = lax.axis_size("seq")
    groups = (cluster_ids // 2).reshape(-1)
    group_hits = (groups[:, None] == jnp.arange(shards, dtype=jnp.int32)[None, :]).astype(jnp.int32)
    earlier = jnp.cumsum(group_hits, axis=0) - group_hits
    buffer_slot = groups * 8 + jnp.sum(earlier * group_hits, axis=1)
    targets = (cluster_ids % 2 * CLUSTER_SIZE + slots).reshape(-1)
    routing = jnp.full((shards * 8,), -1, jnp.int32).at[buffer_slot].set(targets)
    lines = lax.dynamic_index_in_dim(
        routing.reshape(4, HEADS, 2, 32), lax.axis_index("head"), axis=1, keepdims=False
    )
    lines = jnp.pad(lines.reshape(PEERS, 32), ((0, 0), (0, 96)))
    slot_rows = buffer_slot.reshape(tok_rows, 2).T.reshape(4, 128)
    notes = jnp.concatenate([slot_rows, lines], axis=0)[:, None, :]

    def by_head(rows_in):
        return rows_in.reshape(tok_rows, HEADS, HEAD_DIM).transpose(1, 0, 2)

    sent = jnp.concatenate([by_head(a) for a in (queries, keys, values, out_grad)], axis=2)
    arrived, held_notes, held_lines = spread(sent, notes)
    lines_in = (
        held_lines[:, :, 0, :32]
        .reshape(PEERS, RING // 2, 2, 4, 8)
        .transpose(3, 0, 1, 2, 4)
        .reshape(4, 1, 1024)
    )
    boxes, sums = attend_groups(lines_in, arrived)
    rows_back, means = collect(boxes, held_notes, sums)
    back = rows_back.reshape(HEADS, tok_rows, 4, HEAD_DIM)
    outs = tuple(
        back[:, :, i].transpose(1, 0, 2).reshape(tok_rows, HEADS * HEAD_DIM) for i in range(4)
    )
    return outs + (means[:2],)


def solution(mesh):
    placed = (
        P("seq", "head"),
        P("seq", "head"),
        P("seq", "head"),
        P("seq", "head"),
        P("seq", None),
        P("seq", None),
    )
    return jax.shard_map(
        local,
        mesh=mesh,
        in_specs=placed,
        out_specs=(
            P("seq", "head"),
            P("seq", "head"),
            P("seq", "head"),
            P("seq", "head"),
            P("seq", None),
        ),
        check_vma=False,
    )
```

```python
import functools
import math

import jax
import jax.numpy as jnp
from jax import lax
from jax.experimental import pallas as pl
from jax.experimental.pallas import tpu as pltpu
from jax.sharding import PartitionSpec as P

HEAD_DIM = 128
CLUSTER_SIZE = 256
RING = 16
HEADS = 4
PEERS = 8
MESH = pl.DeviceIdType.MESH
OUTWARD = (0, 1, -2, -1, 2, 3, 4, -3)
RETURN = (4, 3, -2, -3, 2, 1, 0, -1)
AHEAD = 3
BACK_AHEAD = 8


def place():
    me = lax.axis_index("seq")
    head = lax.axis_index("head")
    return (me, head, me // (2 * RING), lax.rem(me // 2, RING), lax.rem(me, 2))


def device_at(column, height, core):
    return (column * RING + height) * 2 + core


def around(value, size):
    return lax.rem(value + size, size)


def signal(barrier, seq, head):
    pl.semaphore_signal(barrier, inc=1, device_id=(seq, head), device_id_type=MESH)


def remote(source, target, send_sem, recv_sem, seq, head):
    return pltpu.make_async_remote_copy(
        src_ref=source,
        dst_ref=target,
        send_sem=send_sem,
        recv_sem=recv_sem,
        device_id=(seq, head),
        device_id_type=MESH,
    )


def loop(first, last, body):
    def step(index, carry):
        body(index)
        return carry

    lax.fori_loop(first, last, step, 0)


def hit_table(notes_ref, pair, head):
    shape = (512, 512)
    row = lax.broadcasted_iota(jnp.int32, shape, 0)
    lane = lax.broadcasted_iota(jnp.int32, shape, 1)
    peer = row // 64
    device = ((peer // 2) * HEADS + head) * 2 + peer % 2
    wanted = (device * 4 + row // 16 % 4) * 8 + row % 8
    copies = [
        jnp.concatenate(
            [notes_ref[pair * 2 + side, 2 * c + part] for side in range(2) for part in range(2)],
            axis=1,
        )
        for c in range(2)
    ]
    hit = (copies[0] == wanted) | (copies[1] == wanted)
    same = row // 8 % 2 == lane // 256
    return jnp.where(hit & same, 1.0, 0.0).astype(jnp.bfloat16)


def spread_kernel(
    rows_ref, notes_ref, boxes_ref, held_notes_ref, lines_ref,
    spread_rows, full, packed, note_send, note_recv, line_send, line_recv, line_own,
    first_send, first_recv, stay_sem, z_send, z_recv, y_send, y_recv, x_send, x_recv, own_sem,
):
    me, head, column, height, core = place()
    mine = column * 2 + core
    barrier = pltpu.get_barrier_semaphore()

    def greet_ring(step):
        signal(barrier, device_at(column, lax.rem(height + step, RING), core), head)

    loop(1, RING, greet_ring)

    def greet_peer(step):
        peer = lax.rem(mine + step, PEERS)
        signal(barrier, device_at(peer // 2, height, lax.rem(peer, 2)), head)

    loop(1, PEERS, greet_peer)
    for step in range(1, HEADS):
        signal(barrier, me, lax.rem(head + step, HEADS))
    other = lax.rem(head + 1, HEADS)
    held_notes_ref[height] = notes_ref[...]
    pl.semaphore_wait(barrier, RING - 1 + PEERS - 1 + HEADS - 1)

    def send_notes(step):
        peer = device_at(column, lax.rem(height + step, RING), core)
        remote(notes_ref, held_notes_ref.at[height], note_send, note_recv, peer, head).start()

    def first_copy(quad, step):
        there = lax.rem(head + step, HEADS)
        return remote(
            rows_ref.at[quad, pl.ds(pl.multiple_of(there * 64, 64), 64)],
            spread_rows.at[head, quad],
            first_send,
            first_recv.at[head, quad],
            me,
            there,
        )

    for step in (0, 3, 2, 1):
        quad = lax.rem(height // 4 + step, 4)
        for way in range(1, HEADS):
            first_copy(quad, way).start()
        own = rows_ref.at[quad, pl.ds(pl.multiple_of(head * 64, 64), 64)]
        pltpu.make_async_copy(own, spread_rows.at[head, quad], first_recv.at[head, quad]).start()

    def stay_copy():
        return pltpu.make_async_copy(
            spread_rows.at[lax.rem(height, HEADS), height // 4], full.at[height, head], stay_sem
        )

    def send_quarters(turn):
        there = lax.rem(height // 2 - OUTWARD[turn] + 8, 8)

        def send_quarter(side):
            plane = there * 2 + side
            row_head, quad = (lax.rem(plane, HEADS), plane // 4)
            source = spread_rows.at[row_head, quad]
            pltpu.make_async_copy(source, source, first_recv.at[row_head, quad]).wait()

            @pl.when(plane == height)
            def _():
                stay_copy().start()

            @pl.when(plane != height)
            def _():
                remote(
                    source, full.at[height, head], z_send, z_recv.at[height],
                    device_at(column, plane, core), head,
                ).start()

        loop(0, 2, send_quarter)

    for turn in range(AHEAD):
        send_quarters(turn)
    loop(1, RING, send_notes)

    def y_copy(source, quarter, step, kind):
        part = full.at[source, around(quarter, HEADS)]
        return remote(
            part, part, y_send, y_recv.at[kind, source], me, around(head + step, HEADS)
        )

    def pair_at(turn):
        return lax.rem(height // 2 + OUTWARD[turn] + 8, 8)

    def share(turn):
        for side in range(2):
            source = pair_at(turn) * 2 + side
            part = full.at[source, head]

            @pl.when(source == height)
            def _():
                stay_copy().wait()

            @pl.when(source != height)
            def _():
                remote(part, part, z_send, z_recv.at[source], me, other).wait_recv()

            y_copy(source, head, 1, 0).start()
            y_copy(source, head, -1, 1).start()

    def relay(turn):
        for side in range(2):
            source = pair_at(turn) * 2 + side
            if side == 0:
                y_copy(source, head - 1, 1, 0).wait_recv()
                y_copy(source, head - 1, 1, 2).start()
                y_copy(source, head + 1, -1, 1).wait_recv()
            else:
                y_copy(source, head + 1, -1, 1).wait_recv()
                y_copy(source, head + 1, -1, 2).start()
                y_copy(source, head - 1, 1, 0).wait_recv()

    def deliver(turn):
        pair = pair_at(turn)
        for side in range(2):
            y_copy(pair * 2 + side, head + 2, 1, 2).wait_recv()
        table = hit_table(held_notes_ref, pair, head)
        tokens = full[pl.ds(pair * 2, 2)].reshape(512, 512)
        result = jnp.dot(table, tokens, preferred_element_type=jnp.float32)
        packed[turn] = result.astype(jnp.bfloat16).reshape(PEERS, 4, 16, 512)
        target = boxes_ref.at[mine * 8 + pair]
        pltpu.make_async_copy(packed.at[turn, mine], target, own_sem.at[turn]).start()

        def send(step):
            peer = lax.rem(mine + step, PEERS)
            remote(
                packed.at[turn, peer], target, x_send, x_recv,
                device_at(peer // 2, height, lax.rem(peer, 2)), head,
            ).start()

        loop(1, PEERS, send)

    def send_lines(step):
        peer = lax.rem(mine + step, PEERS)
        remote(
            held_notes_ref.at[pl.ds(0, RING), 4 + peer], lines_ref.at[mine], line_send, line_recv,
            device_at(peer // 2, height, lax.rem(peer, 2)), head,
        ).start()

    own_lines = pltpu.make_async_copy(
        held_notes_ref.at[pl.ds(0, RING), 4 + mine], lines_ref.at[mine], line_own
    )
    for turn in range(10):
        if turn < 8:
            share(turn)
        if turn + AHEAD < 8:
            send_quarters(turn + AHEAD)
        if 1 <= turn < 9:
            relay(turn - 1)
        if turn == 2:
            lot = held_notes_ref.at[pl.ds(0, RING - 1)]
            remote(lot, lot, note_send, note_recv, me, other).wait()
            own_lines.start()
            loop(1, PEERS, send_lines)
        if turn >= 2:
            deliver(turn - 2)
    for turn in range(8):
        pltpu.make_async_copy(
            packed.at[turn, mine], boxes_ref.at[mine * 8 + turn], own_sem.at[turn]
        ).wait()
    lot = boxes_ref.at[pl.ds(0, 56)]
    remote(lot, lot, x_send, x_recv, me, other).wait()
    own_lines.wait()
    lot = lines_ref.at[pl.ds(0, PEERS - 1)]
    remote(lot, lot, line_send, line_recv, me, other).wait()
    lot = full.at[pl.ds(0, 12)]
    remote(lot, lot, y_send, y_recv.at[0, 0], me, other).wait_send()

    def sent_quarter(index):
        part = full.at[0, 0]
        remote(part, part, z_send, z_recv.at[0], me, other).wait_send()

    loop(0, RING - 1, sent_quarter)
    lot = spread_rows.at[pl.ds(0, HEADS - 1)]
    remote(lot, lot, first_send, first_recv.at[0, 0], me, other).wait_send()


def spread(rows, notes):
    vmem = pl.BlockSpec(memory_space=pltpu.VMEM)
    dma = pltpu.SemaphoreType.DMA
    return pl.pallas_call(
        spread_kernel,
        out_shape=(
            jax.ShapeDtypeStruct((64, 4, 16, 512), jnp.bfloat16),
            jax.ShapeDtypeStruct((RING,) + notes.shape, jnp.int32),
            jax.ShapeDtypeStruct((PEERS, RING) + notes.shape[1:], jnp.int32),
        ),
        in_specs=[vmem] * 2,
        out_specs=(vmem,) * 3,
        scratch_shapes=[
            pltpu.VMEM((HEADS, 4, 64, 512), jnp.bfloat16),
            pltpu.VMEM((RING, 4, 64, 512), jnp.bfloat16),
            pltpu.VMEM((8, PEERS, 4, 16, 512), jnp.bfloat16),
            dma, dma, dma, dma, dma,
            dma, dma((HEADS, 4)), dma,
            dma, dma((RING,)), dma, dma((3, RING)), dma, dma, dma((8,)),
        ],
        compiler_params=pltpu.CompilerParams(
            collective_id=0, has_side_effects=True, vmem_limit_bytes=48 * 2**20
        ),
    )(rows, notes)


def product(left, right, left_dim, right_dim):
    return lax.dot_general(
        left, right, (((left_dim,), (right_dim,)), ((), ())), preferred_element_type=jnp.float32
    )


def attend_kernel(lines_ref, rows_ref, boxes_ref, sums_ref, results):
    scale = 1.0 / math.sqrt(HEAD_DIM)
    shape = (512, 1024)
    row = lax.broadcasted_iota(jnp.int32, shape, 0)
    table = jnp.where(lines_ref[0] == row, 1.0, 0.0).astype(jnp.bfloat16)
    grouped = product(table, rows_ref[...].reshape(1024, 512), 1, 0).astype(jnp.bfloat16)
    size = (CLUSTER_SIZE, CLUSTER_SIZE)
    allowed = lax.broadcasted_iota(jnp.int32, size, 1) <= lax.broadcasted_iota(jnp.int32, size, 0)
    sums_ref[...] = jnp.zeros_like(sums_ref)
    for cluster in range(2):
        first = cluster * CLUSTER_SIZE
        query, key, value, grad = (
            grouped[first : first + CLUSTER_SIZE, i * HEAD_DIM : (i + 1) * HEAD_DIM]
            for i in range(4)
        )
        scores = jnp.where(allowed, product(query, key, 1, 1) * scale, jnp.float32(-1e30))
        weights = jnp.exp(scores - jnp.max(scores, axis=1, keepdims=True))
        attention = weights / jnp.sum(weights, axis=1, keepdims=True)
        attn_low = attention.astype(jnp.bfloat16)
        prob_grad = product(grad, value, 1, 1)
        row_dot = jnp.sum(attention * prob_grad, axis=1, keepdims=True)
        grad_score = (attention * (prob_grad - row_dot) * scale).astype(jnp.bfloat16)
        outs = (
            product(attn_low, value, 1, 0),
            product(grad_score, key, 1, 0),
            product(grad_score, query, 0, 0),
            product(attn_low, grad, 0, 0),
        )
        for i, out in enumerate(outs):
            results[first : first + CLUSTER_SIZE, i * HEAD_DIM : (i + 1) * HEAD_DIM] = out.astype(
                jnp.bfloat16
            )
        key_float = key.astype(jnp.float32)
        normed = key_float * lax.rsqrt(
            jnp.mean(key_float * key_float, axis=1, keepdims=True) + 1e-06
        )
        sums_ref[0, cluster : cluster + 1] = jnp.sum(normed, axis=0, keepdims=True)
    boxes = product(table, results[...], 0, 0)
    boxes_ref[...] = boxes.astype(jnp.bfloat16).reshape(64, 1, 16, 512)


def attend_groups(lines, boxes):
    box_spec = pl.BlockSpec((64, 1, 16, 512), lambda group: (0, group, 0, 0))
    return pl.pallas_call(
        attend_kernel,
        grid=(4,),
        out_shape=(
            jax.ShapeDtypeStruct(boxes.shape, jnp.bfloat16),
            jax.ShapeDtypeStruct((4, 8, HEAD_DIM), jnp.float32),
        ),
        in_specs=[pl.BlockSpec((1, 1, 1024), lambda group: (group, 0, 0)), box_spec],
        out_specs=(box_spec, pl.BlockSpec((1, 8, HEAD_DIM), lambda group: (group, 0, 0))),
        scratch_shapes=[pltpu.VMEM((512, 512), jnp.bfloat16)],
        compiler_params=pltpu.CompilerParams(vmem_limit_bytes=48 * 2**20),
    )(lines, boxes)


def collect_kernel(
    boxes_ref, held_notes_ref, sums_ref, rows_ref, means_ref,
    held, part, far, near, done, sums, x_send, x_recv, own_sem,
    y_send, far_recv, near_recv, z_send, z_recv, sum_send, sum_recv,
):
    me, head, column, height, core = place()
    mine = column * 2 + core
    here = lax.rem(height, HEADS) == head
    owner = (height // 4 == head) & (lax.rem(height // 2, 2) == core)
    barrier = pltpu.get_barrier_semaphore()

    def greet_peer(step):
        peer = lax.rem(mine + step, PEERS)
        signal(barrier, device_at(peer // 2, height, lax.rem(peer, 2)), head)

    loop(1, PEERS, greet_peer)
    for step in (1, HEADS - 1):
        signal(barrier, me, lax.rem(head + step, HEADS))

    def greet_relay(index):
        plane = index // 4 * 4 + head
        quarter = lax.rem(index, 4)

        @pl.when(jnp.logical_not((plane == height) & (quarter == head)))
        def _():
            signal(barrier, device_at(column, plane, core), quarter)

    loop(0, RING, greet_relay)

    def greet_summer(plane):
        @pl.when(jnp.logical_not(owner & (plane == height)))
        def _():
            signal(barrier, device_at(column, plane, lax.rem(height // 2, 2)), height // 4)

    loop(0, RING, greet_summer)
    pl.semaphore_wait(
        barrier, PEERS - 1 + 2 + 2 * RING - jnp.where(here, 1, 0) - jnp.where(owner, 1, 0)
    )

    def pair_at(turn):
        return lax.rem(height // 2 + RETURN[turn] + 8, 8)

    def send_boxes(turn):
        pair = pair_at(turn)
        pltpu.make_async_copy(
            boxes_ref.at[mine * 8 + pair], held.at[pair, mine], own_sem.at[turn]
        ).start()

        def send_box(step):
            peer = lax.rem(mine + step, PEERS)
            remote(
                boxes_ref.at[peer * 8 + pair], held.at[pair, mine], x_send, x_recv.at[pair],
                device_at(peer // 2, height, lax.rem(peer, 2)), head,
            ).start()

        loop(1, PEERS, send_box)

    for turn in range(BACK_AHEAD):
        send_boxes(turn)

    def send_sum(index):
        group = index // 4
        there = lax.rem(head + index, HEADS)
        peer = device_at(column, (head * 2 + core) * 2 + group // 2, lax.rem(group, 2))
        stays = (peer == me) & (there == head)

        @pl.when(stays)
        def _():
            pltpu.make_async_copy(sums_ref.at[group], sums.at[height], sum_recv).start()

        @pl.when(jnp.logical_not(stays))
        def _():
            remote(
                sums_ref.at[group], sums.at[height], sum_send, sum_recv, peer, there
            ).start()

    loop(0, RING, send_sum)

    def up(source, quarter, target, recv):
        return remote(
            part.at[source, around(quarter, HEADS)], target, y_send, recv, me,
            around(head + 1, HEADS),
        )

    def down(source, quarter, target, recv):
        return remote(
            part.at[source, around(quarter, HEADS)], target, y_send, recv, me,
            around(head - 1, HEADS),
        )

    def unpack(turn):
        pair = pair_at(turn)
        pltpu.make_async_copy(
            boxes_ref.at[mine * 8 + pair], held.at[pair, mine], own_sem.at[turn]
        ).wait()
        lot = held.at[pair, pl.ds(0, PEERS - 1)]
        remote(lot, lot, x_send, x_recv.at[pair], me, around(head + 1, HEADS)).wait_recv()
        table = hit_table(held_notes_ref, pair, head)
        result = lax.dot_general(
            table, held[pair].reshape(512, 512), (((0,), (0,)), ((), ())),
            preferred_element_type=jnp.float32,
        )
        part[pl.ds(pair * 2, 2)] = result.astype(jnp.bfloat16).reshape(2, 4, 64, 512)
        even, odd = (pair * 2, pair * 2 + 1)
        up(even, head + 2, far.at[even], far_recv.at[even]).start()
        down(even, head - 1, near.at[1, even], near_recv.at[1, even]).start()
        down(odd, head + 2, far.at[odd], far_recv.at[odd]).start()
        up(odd, head + 1, near.at[0, odd], near_recv.at[0, odd]).start()

    def join(turn):
        even = pair_at(turn) * 2
        for source, step in ((even, 1), (even + 1, -1)):
            spot = around(head + step, HEADS)
            up(source, head + step, far.at[source], far_recv.at[source]).wait_recv()
            total = part[source, spot].astype(jnp.float32) + far[source].astype(jnp.float32)
            part[source, spot] = total.astype(jnp.bfloat16)
            if step == 1:
                up(source, head + 1, near.at[0, source], near_recv.at[0, source]).start()
            else:
                down(source, head - 1, near.at[1, source], near_recv.at[1, source]).start()

    def finish(turn):
        for side in range(2):
            source = pair_at(turn) * 2 + side
            total = part[source, head].astype(jnp.float32)
            for way in range(2):
                up(source, head, near.at[way, source], near_recv.at[way, source]).wait_recv()
                total += near[way, source].astype(jnp.float32)
            done[source] = total.astype(jnp.bfloat16)
            target = rows_ref.at[height // 4, head]
            stays = here & (source == height)

            @pl.when(stays)
            def _():
                pltpu.make_async_copy(done.at[source], target, z_recv).start()

            @pl.when(jnp.logical_not(stays))
            def _():
                remote(
                    done.at[source], target, z_send, z_recv,
                    device_at(column, source, core), lax.rem(height, HEADS),
                ).start()

    for turn in range(10):
        if turn < 8:
            unpack(turn)
        if turn + BACK_AHEAD < 8:
            send_boxes(turn + BACK_AHEAD)
        if 1 <= turn < 9:
            join(turn - 1)
        if turn >= 2:
            finish(turn - 2)
    other = around(head + 1, HEADS)
    remote(sums, sums, sum_send, sum_recv, me, other).wait_recv()
    grand = sums[0]
    for plane in range(1, RING):
        grand += sums[plane]
    means_ref[...] = grand * lax.rsqrt(jnp.mean(grand * grand, axis=1, keepdims=True) + 1e-06)
    lot = boxes_ref.at[pl.ds(0, 56)]
    remote(lot, lot, x_send, x_recv.at[0], me, other).wait_send()
    lot = part.at[pl.ds(0, 12)]
    remote(lot, lot, y_send, far_recv.at[0], me, other).wait_send()

    def sent_sum(index):
        remote(sums.at[0], sums.at[0], sum_send, sum_recv, me, other).wait_send()

    loop(0, RING - jnp.where(owner, 1, 0), sent_sum)

    def sent_rows(index):
        remote(done.at[0], done.at[0], z_send, z_recv, me, other).wait_send()

    loop(0, RING - jnp.where(here, 1, 0), sent_rows)
    remote(rows_ref, rows_ref, z_send, z_recv, me, other).wait_recv()


def collect(boxes, held_notes, sums):
    vmem = pl.BlockSpec(memory_space=pltpu.VMEM)
    dma = pltpu.SemaphoreType.DMA
    return pl.pallas_call(
        collect_kernel,
        out_shape=(
            jax.ShapeDtypeStruct((4, 4, 64, 512), jnp.bfloat16),
            jax.ShapeDtypeStruct(sums.shape[1:], jnp.float32),
        ),
        in_specs=[vmem] * 3,
        out_specs=(vmem,) * 2,
        scratch_shapes=[
            pltpu.VMEM((8, PEERS, 4, 16, 512), jnp.bfloat16),
            pltpu.VMEM((RING, 4, 64, 512), jnp.bfloat16),
            pltpu.VMEM((RING, 64, 512), jnp.bfloat16),
            pltpu.VMEM((2, RING, 64, 512), jnp.bfloat16),
            pltpu.VMEM((RING, 64, 512), jnp.bfloat16),
            pltpu.VMEM((RING,) + sums.shape[1:], jnp.float32),
            dma, dma((8,)), dma((8,)),
            dma, dma((RING,)), dma((2, RING)), dma, dma, dma, dma,
        ],
        compiler_params=pltpu.CompilerParams(
            collective_id=1, has_side_effects=True, vmem_limit_bytes=48 * 2**20
        ),
    )(boxes, held_notes, sums)


def prepare_kernel(
    queries_ref, keys_ref, values_ref, grads_ref, ids_ref, slots_ref, rows_ref, notes_ref
):
    head = lax.axis_index("head")
    for i, source in enumerate((queries_ref, keys_ref, values_ref, grads_ref)):
        for quad in range(HEADS):
            rows_ref[quad, :, i * HEAD_DIM : (i + 1) * HEAD_DIM] = source[
                :, quad * HEAD_DIM : (quad + 1) * HEAD_DIM
            ]
    count = ids_ref.shape[0]
    copies = 2 * count

    def iota(shape, dim):
        return lax.broadcasted_iota(jnp.int32, shape, dim)

    def ones_where(condition):
        return jnp.where(condition, 1.0, 0.0).astype(jnp.bfloat16)

    square = (count, count)
    unit = ones_where(iota(square, 0) == iota(square, 1))

    def as_row(column_ref):
        turned = product(column_ref[...].astype(jnp.float32).astype(jnp.bfloat16), unit, 0, 0)
        return jnp.concatenate([turned[0:1], turned[1:2]], axis=1)

    ids = as_row(ids_ref).astype(jnp.int32)
    slots = as_row(slots_ref)
    groups = ids // 2
    hit = iota((128, copies), 0) == groups
    before = ones_where(iota((copies, copies), 0) < iota((copies, copies), 1))
    earlier = product(ones_where(hit), before, 1, 0)
    rank = jnp.sum(jnp.where(hit, earlier, 0.0), axis=0, keepdims=True)
    spots = groups * 8 + rank.astype(jnp.int32)
    shape = (PEERS * 128, copies)
    row = iota(shape, 0)
    peer, line = (row // 128, row % 128)
    device = ((peer // 2) * HEADS + head) * 2 + peer % 2
    wanted = jnp.where(line < 32, device * 32 + line, -1)
    kind = iota((8, copies), 0)
    local_ids = (ids % 2).astype(jnp.float32)
    facts = jnp.where(
        kind == 0, slots, jnp.where(kind == 1, local_ids, jnp.where(kind == 2, 1.0, 0.0))
    ).astype(jnp.bfloat16)
    found = product(facts, ones_where(spots == wanted), 1, 1)
    lines = (found[0:1] + CLUSTER_SIZE * found[1:2] + found[2:3] - 1.0).astype(jnp.int32)
    for part in range(4):
        notes_ref[part] = spots[:, part * 128 : (part + 1) * 128]
    for part in range(PEERS):
        notes_ref[4 + part] = lines[:, part * 128 : (part + 1) * 128]


def finish_kernel(rows_ref, means_in_ref, out_ref, query_ref, key_ref, value_ref, means_ref):
    for quad in range(HEADS):
        rows = rows_ref[quad].reshape(256, 512)
        for i, target in enumerate((out_ref, query_ref, key_ref, value_ref)):
            target[:, quad * HEAD_DIM : (quad + 1) * HEAD_DIM] = rows[
                :, i * HEAD_DIM : (i + 1) * HEAD_DIM
            ]
    means_ref[...] = means_in_ref[0:2]


def local(queries, keys, values, out_grad, cluster_ids, slots):
    vmem = pl.BlockSpec(memory_space=pltpu.VMEM)
    params = pltpu.CompilerParams(vmem_limit_bytes=32 * 2**20)
    sent, notes = pl.pallas_call(
        prepare_kernel,
        out_shape=(
            jax.ShapeDtypeStruct((HEADS, 256, 512), jnp.bfloat16),
            jax.ShapeDtypeStruct((4 + PEERS, 1, 128), jnp.int32),
        ),
        in_specs=[vmem] * 6,
        out_specs=(vmem,) * 2,
        compiler_params=params,
    )(queries, keys, values, out_grad, cluster_ids, slots)
    arrived, held_notes, held_lines = spread(sent, notes)
    lines_in = (
        held_lines[:, :, 0, :32]
        .reshape(PEERS, RING // 2, 2, 4, 8)
        .transpose(3, 0, 1, 2, 4)
        .reshape(4, 1, 1024)
    )
    boxes, sums = attend_groups(lines_in, arrived)
    rows_back, means = collect(boxes, held_notes, sums)
    whole = jax.ShapeDtypeStruct(queries.shape, jnp.bfloat16)
    return pl.pallas_call(
        finish_kernel,
        out_shape=(whole,) * 4 + (jax.ShapeDtypeStruct((2, HEAD_DIM), jnp.float32),),
        in_specs=[vmem] * 2,
        out_specs=(vmem,) * 5,
        compiler_params=params,
    )(rows_back, means)


def solution(mesh):
    placed = (
        P("seq", "head"),
        P("seq", "head"),
        P("seq", "head"),
        P("seq", "head"),
        P("seq", None),
        P("seq", None),
    )
    return jax.shard_map(
        local,
        mesh=mesh,
        in_specs=placed,
        out_specs=(
            P("seq", "head"),
            P("seq", "head"),
            P("seq", "head"),
            P("seq", "head"),
            P("seq", None),
        ),
        check_vma=False,
    )
```

```python
import functools
import math

import jax
import jax.numpy as jnp
from jax import lax
from jax.experimental import pallas as pl
from jax.experimental.pallas import tpu as pltpu
from jax.sharding import PartitionSpec as P

HEAD_DIM = 128
CLUSTER_SIZE = 256
RING = 16
HEADS = 4
PEERS = 8
MESH = pl.DeviceIdType.MESH
OUTWARD = (0, 1, -1, 2, -2, 3, -3, 4)
RETURN = (4, 3, -2, -3, 2, 1, 0, -1)
AHEAD = 3
BACK_AHEAD = 8


def place():
    me = lax.axis_index("seq")
    head = lax.axis_index("head")
    return (me, head, me // (2 * RING), lax.rem(me // 2, RING), lax.rem(me, 2))


def device_at(column, height, core):
    return (column * RING + height) * 2 + core


def around(value, size):
    return lax.rem(value + size, size)


def signal(barrier, seq, head):
    pl.semaphore_signal(barrier, inc=1, device_id=(seq, head), device_id_type=MESH)


def remote(source, target, send_sem, recv_sem, seq, head):
    return pltpu.make_async_remote_copy(
        src_ref=source,
        dst_ref=target,
        send_sem=send_sem,
        recv_sem=recv_sem,
        device_id=(seq, head),
        device_id_type=MESH,
    )


def loop(first, last, body):
    def step(index, carry):
        body(index)
        return carry

    lax.fori_loop(first, last, step, 0)


def hit_table(notes_ref, pair, head):
    shape = (512, 512)
    row = lax.broadcasted_iota(jnp.int32, shape, 0)
    lane = lax.broadcasted_iota(jnp.int32, shape, 1)
    peer = row // 64
    device = ((peer // 2) * HEADS + head) * 2 + peer % 2
    wanted = (device * 4 + row // 16 % 4) * 8 + row % 8
    copies = [
        jnp.concatenate(
            [notes_ref[pair * 2 + side, 2 * c + part] for side in range(2) for part in range(2)],
            axis=1,
        )
        for c in range(2)
    ]
    hit = (copies[0] == wanted) | (copies[1] == wanted)
    same = row // 8 % 2 == lane // 256
    return jnp.where(hit & same, 1.0, 0.0).astype(jnp.bfloat16)


def spread_kernel(
    rows_ref, notes_ref, boxes_ref, held_notes_ref, lines_ref,
    spread_rows, full, packed, note_send, note_recv, line_send, line_recv, line_own,
    first_send, first_recv, stay_sem, z_send, z_recv, y_send, y_recv, x_send, x_recv, own_sem,
):
    me, head, column, height, core = place()
    mine = column * 2 + core
    barrier = pltpu.get_barrier_semaphore()

    def greet_ring(step):
        signal(barrier, device_at(column, lax.rem(height + step, RING), core), head)

    loop(1, RING, greet_ring)

    def greet_peer(step):
        peer = lax.rem(mine + step, PEERS)
        signal(barrier, device_at(peer // 2, height, lax.rem(peer, 2)), head)

    loop(1, PEERS, greet_peer)
    for step in range(1, HEADS):
        signal(barrier, me, lax.rem(head + step, HEADS))
    other = lax.rem(head + 1, HEADS)
    held_notes_ref[height] = notes_ref[...]
    pl.semaphore_wait(barrier, RING - 1 + PEERS - 1 + HEADS - 1)

    def send_notes(step):
        peer = device_at(column, lax.rem(height + step, RING), core)
        remote(notes_ref, held_notes_ref.at[height], note_send, note_recv, peer, head).start()

    def first_copy(quad, step):
        there = lax.rem(head + step, HEADS)
        return remote(
            rows_ref.at[quad, pl.ds(pl.multiple_of(there * 64, 64), 64)],
            spread_rows.at[head, quad],
            first_send,
            first_recv.at[head, quad],
            me,
            there,
        )

    for step in (0, 3, 2, 1):
        quad = lax.rem(height // 4 + step, 4)
        for way in range(1, HEADS):
            first_copy(quad, way).start()
        own = rows_ref.at[quad, pl.ds(pl.multiple_of(head * 64, 64), 64)]
        pltpu.make_async_copy(own, spread_rows.at[head, quad], first_recv.at[head, quad]).start()

    def stay_copy():
        return pltpu.make_async_copy(
            spread_rows.at[lax.rem(height, HEADS), height // 4], full.at[height, head], stay_sem
        )

    def send_quarters(turn):
        there = lax.rem(height // 2 - OUTWARD[turn] + 8, 8)

        def send_quarter(side):
            plane = there * 2 + side
            row_head, quad = (lax.rem(plane, HEADS), plane // 4)
            source = spread_rows.at[row_head, quad]
            pltpu.make_async_copy(source, source, first_recv.at[row_head, quad]).wait()

            @pl.when(plane == height)
            def _():
                stay_copy().start()

            @pl.when(plane != height)
            def _():
                remote(
                    source, full.at[height, head], z_send, z_recv.at[height],
                    device_at(column, plane, core), head,
                ).start()

        loop(0, 2, send_quarter)

    for turn in range(AHEAD):
        send_quarters(turn)
    loop(1, RING, send_notes)

    def y_copy(source, quarter, step, kind):
        part = full.at[source, around(quarter, HEADS)]
        return remote(
            part, part, y_send, y_recv.at[kind, source], me, around(head + step, HEADS)
        )

    def pair_at(turn):
        return lax.rem(height // 2 + OUTWARD[turn] + 8, 8)

    def share(turn):
        for side in range(2):
            source = pair_at(turn) * 2 + side
            part = full.at[source, head]

            @pl.when(source == height)
            def _():
                stay_copy().wait()

            @pl.when(source != height)
            def _():
                remote(part, part, z_send, z_recv.at[source], me, other).wait_recv()

            y_copy(source, head, 1, 0).start()
            y_copy(source, head, -1, 1).start()

    def relay(turn):
        for side in range(2):
            source = pair_at(turn) * 2 + side
            if side == 0:
                y_copy(source, head - 1, 1, 0).wait_recv()
                y_copy(source, head - 1, 1, 2).start()
                y_copy(source, head + 1, -1, 1).wait_recv()
            else:
                y_copy(source, head + 1, -1, 1).wait_recv()
                y_copy(source, head + 1, -1, 2).start()
                y_copy(source, head - 1, 1, 0).wait_recv()

    def deliver(turn):
        pair = pair_at(turn)
        for side in range(2):
            y_copy(pair * 2 + side, head + 2, 1, 2).wait_recv()
        table = hit_table(held_notes_ref, pair, head)
        tokens = full[pl.ds(pair * 2, 2)].reshape(512, 512)
        result = jnp.dot(table, tokens, preferred_element_type=jnp.float32)
        packed[turn] = result.astype(jnp.bfloat16).reshape(PEERS, 4, 16, 512)
        target = boxes_ref.at[mine * 8 + pair]
        pltpu.make_async_copy(packed.at[turn, mine], target, own_sem.at[turn]).start()

        def send(step):
            peer = lax.rem(mine + step, PEERS)
            remote(
                packed.at[turn, peer], target, x_send, x_recv,
                device_at(peer // 2, height, lax.rem(peer, 2)), head,
            ).start()

        loop(1, PEERS, send)

    def send_lines(step):
        peer = lax.rem(mine + step, PEERS)
        remote(
            held_notes_ref.at[pl.ds(0, RING), 4 + peer], lines_ref.at[mine], line_send, line_recv,
            device_at(peer // 2, height, lax.rem(peer, 2)), head,
        ).start()

    own_lines = pltpu.make_async_copy(
        held_notes_ref.at[pl.ds(0, RING), 4 + mine], lines_ref.at[mine], line_own
    )
    for turn in range(10):
        if turn < 8:
            share(turn)
        if turn + AHEAD < 8:
            send_quarters(turn + AHEAD)
        if 1 <= turn < 9:
            relay(turn - 1)
        if turn == 2:
            lot = held_notes_ref.at[pl.ds(0, RING - 1)]
            remote(lot, lot, note_send, note_recv, me, other).wait()
            own_lines.start()
            loop(1, PEERS, send_lines)
        if turn >= 2:
            deliver(turn - 2)
    for turn in range(8):
        pltpu.make_async_copy(
            packed.at[turn, mine], boxes_ref.at[mine * 8 + turn], own_sem.at[turn]
        ).wait()
    lot = boxes_ref.at[pl.ds(0, 56)]
    remote(lot, lot, x_send, x_recv, me, other).wait()
    own_lines.wait()
    lot = lines_ref.at[pl.ds(0, PEERS - 1)]
    remote(lot, lot, line_send, line_recv, me, other).wait()
    lot = full.at[pl.ds(0, 12)]
    remote(lot, lot, y_send, y_recv.at[0, 0], me, other).wait_send()

    def sent_quarter(index):
        part = full.at[0, 0]
        remote(part, part, z_send, z_recv.at[0], me, other).wait_send()

    loop(0, RING - 1, sent_quarter)
    lot = spread_rows.at[pl.ds(0, HEADS - 1)]
    remote(lot, lot, first_send, first_recv.at[0, 0], me, other).wait_send()


def spread(rows, notes):
    vmem = pl.BlockSpec(memory_space=pltpu.VMEM)
    dma = pltpu.SemaphoreType.DMA
    return pl.pallas_call(
        spread_kernel,
        out_shape=(
            jax.ShapeDtypeStruct((64, 4, 16, 512), jnp.bfloat16),
            jax.ShapeDtypeStruct((RING,) + notes.shape, jnp.int32),
            jax.ShapeDtypeStruct((PEERS, RING) + notes.shape[1:], jnp.int32),
        ),
        in_specs=[vmem] * 2,
        out_specs=(vmem,) * 3,
        scratch_shapes=[
            pltpu.VMEM((HEADS, 4, 64, 512), jnp.bfloat16),
            pltpu.VMEM((RING, 4, 64, 512), jnp.bfloat16),
            pltpu.VMEM((8, PEERS, 4, 16, 512), jnp.bfloat16),
            dma, dma, dma, dma, dma,
            dma, dma((HEADS, 4)), dma,
            dma, dma((RING,)), dma, dma((3, RING)), dma, dma, dma((8,)),
        ],
        compiler_params=pltpu.CompilerParams(
            collective_id=0, has_side_effects=True, vmem_limit_bytes=48 * 2**20
        ),
    )(rows, notes)


def product(left, right, left_dim, right_dim):
    return lax.dot_general(
        left, right, (((left_dim,), (right_dim,)), ((), ())), preferred_element_type=jnp.float32
    )


def attend_kernel(lines_ref, rows_ref, boxes_ref, sums_ref, results):
    scale = 1.0 / math.sqrt(HEAD_DIM)
    shape = (512, 1024)
    row = lax.broadcasted_iota(jnp.int32, shape, 0)
    table = jnp.where(lines_ref[0] == row, 1.0, 0.0).astype(jnp.bfloat16)
    grouped = product(table, rows_ref[...].reshape(1024, 512), 1, 0).astype(jnp.bfloat16)
    size = (CLUSTER_SIZE, CLUSTER_SIZE)
    allowed = lax.broadcasted_iota(jnp.int32, size, 1) <= lax.broadcasted_iota(jnp.int32, size, 0)
    sums_ref[...] = jnp.zeros_like(sums_ref)
    for cluster in range(2):
        first = cluster * CLUSTER_SIZE
        query, key, value, grad = (
            grouped[first : first + CLUSTER_SIZE, i * HEAD_DIM : (i + 1) * HEAD_DIM]
            for i in range(4)
        )
        scores = jnp.where(allowed, product(query, key, 1, 1) * scale, jnp.float32(-1e30))
        weights = jnp.exp(scores - jnp.max(scores, axis=1, keepdims=True))
        attention = weights / jnp.sum(weights, axis=1, keepdims=True)
        attn_low = attention.astype(jnp.bfloat16)
        prob_grad = product(grad, value, 1, 1)
        row_dot = jnp.sum(attention * prob_grad, axis=1, keepdims=True)
        grad_score = (attention * (prob_grad - row_dot) * scale).astype(jnp.bfloat16)
        outs = (
            product(attn_low, value, 1, 0),
            product(grad_score, key, 1, 0),
            product(grad_score, query, 0, 0),
            product(attn_low, grad, 0, 0),
        )
        for i, out in enumerate(outs):
            results[first : first + CLUSTER_SIZE, i * HEAD_DIM : (i + 1) * HEAD_DIM] = out.astype(
                jnp.bfloat16
            )
        key_float = key.astype(jnp.float32)
        normed = key_float * lax.rsqrt(
            jnp.mean(key_float * key_float, axis=1, keepdims=True) + 1e-06
        )
        sums_ref[0, cluster : cluster + 1] = jnp.sum(normed, axis=0, keepdims=True)
    boxes = product(table, results[...], 0, 0)
    boxes_ref[...] = boxes.astype(jnp.bfloat16).reshape(64, 1, 16, 512)


def attend_groups(lines, boxes):
    box_spec = pl.BlockSpec((64, 1, 16, 512), lambda group: (0, group, 0, 0))
    return pl.pallas_call(
        attend_kernel,
        grid=(4,),
        out_shape=(
            jax.ShapeDtypeStruct(boxes.shape, jnp.bfloat16),
            jax.ShapeDtypeStruct((4, 8, HEAD_DIM), jnp.float32),
        ),
        in_specs=[pl.BlockSpec((1, 1, 1024), lambda group: (group, 0, 0)), box_spec],
        out_specs=(box_spec, pl.BlockSpec((1, 8, HEAD_DIM), lambda group: (group, 0, 0))),
        scratch_shapes=[pltpu.VMEM((512, 512), jnp.bfloat16)],
        compiler_params=pltpu.CompilerParams(vmem_limit_bytes=48 * 2**20),
    )(lines, boxes)


def collect_kernel(
    boxes_ref, held_notes_ref, sums_ref, rows_ref, means_ref,
    held, part, far, near, done, sums, x_send, x_recv, own_sem,
    y_send, far_recv, near_recv, z_send, z_recv, sum_send, sum_recv,
):
    me, head, column, height, core = place()
    mine = column * 2 + core
    here = lax.rem(height, HEADS) == head
    owner = (height // 4 == head) & (lax.rem(height // 2, 2) == core)
    barrier = pltpu.get_barrier_semaphore()

    def greet_peer(step):
        peer = lax.rem(mine + step, PEERS)
        signal(barrier, device_at(peer // 2, height, lax.rem(peer, 2)), head)

    loop(1, PEERS, greet_peer)
    for step in (1, HEADS - 1):
        signal(barrier, me, lax.rem(head + step, HEADS))

    def greet_relay(index):
        plane = index // 4 * 4 + head
        quarter = lax.rem(index, 4)

        @pl.when(jnp.logical_not((plane == height) & (quarter == head)))
        def _():
            signal(barrier, device_at(column, plane, core), quarter)

    loop(0, RING, greet_relay)

    def greet_summer(plane):
        @pl.when(jnp.logical_not(owner & (plane == height)))
        def _():
            signal(barrier, device_at(column, plane, lax.rem(height // 2, 2)), height // 4)

    loop(0, RING, greet_summer)
    pl.semaphore_wait(
        barrier, PEERS - 1 + 2 + 2 * RING - jnp.where(here, 1, 0) - jnp.where(owner, 1, 0)
    )

    def pair_at(turn):
        return lax.rem(height // 2 + RETURN[turn] + 8, 8)

    def send_boxes(turn):
        pair = pair_at(turn)
        pltpu.make_async_copy(
            boxes_ref.at[mine * 8 + pair], held.at[pair, mine], own_sem.at[turn]
        ).start()

        def send_box(step):
            peer = lax.rem(mine + step, PEERS)
            remote(
                boxes_ref.at[peer * 8 + pair], held.at[pair, mine], x_send, x_recv.at[pair],
                device_at(peer // 2, height, lax.rem(peer, 2)), head,
            ).start()

        loop(1, PEERS, send_box)

    for turn in range(BACK_AHEAD):
        send_boxes(turn)

    def send_sum(index):
        group = index // 4
        there = lax.rem(head + index, HEADS)
        peer = device_at(column, (head * 2 + core) * 2 + group // 2, lax.rem(group, 2))
        stays = (peer == me) & (there == head)

        @pl.when(stays)
        def _():
            pltpu.make_async_copy(sums_ref.at[group], sums.at[height], sum_recv).start()

        @pl.when(jnp.logical_not(stays))
        def _():
            remote(
                sums_ref.at[group], sums.at[height], sum_send, sum_recv, peer, there
            ).start()

    loop(0, RING, send_sum)

    def up(source, quarter, target, recv):
        return remote(
            part.at[source, around(quarter, HEADS)], target, y_send, recv, me,
            around(head + 1, HEADS),
        )

    def down(source, quarter, target, recv):
        return remote(
            part.at[source, around(quarter, HEADS)], target, y_send, recv, me,
            around(head - 1, HEADS),
        )

    def unpack(turn):
        pair = pair_at(turn)
        pltpu.make_async_copy(
            boxes_ref.at[mine * 8 + pair], held.at[pair, mine], own_sem.at[turn]
        ).wait()
        lot = held.at[pair, pl.ds(0, PEERS - 1)]
        remote(lot, lot, x_send, x_recv.at[pair], me, around(head + 1, HEADS)).wait_recv()
        table = hit_table(held_notes_ref, pair, head)
        result = lax.dot_general(
            table, held[pair].reshape(512, 512), (((0,), (0,)), ((), ())),
            preferred_element_type=jnp.float32,
        )
        part[pl.ds(pair * 2, 2)] = result.astype(jnp.bfloat16).reshape(2, 4, 64, 512)
        even, odd = (pair * 2, pair * 2 + 1)
        up(even, head + 2, far.at[even], far_recv.at[even]).start()
        down(even, head - 1, near.at[1, even], near_recv.at[1, even]).start()
        down(odd, head + 2, far.at[odd], far_recv.at[odd]).start()
        up(odd, head + 1, near.at[0, odd], near_recv.at[0, odd]).start()

    def join(turn):
        even = pair_at(turn) * 2
        for source, step in ((even, 1), (even + 1, -1)):
            spot = around(head + step, HEADS)
            up(source, head + step, far.at[source], far_recv.at[source]).wait_recv()
            total = part[source, spot].astype(jnp.float32) + far[source].astype(jnp.float32)
            part[source, spot] = total.astype(jnp.bfloat16)
            if step == 1:
                up(source, head + 1, near.at[0, source], near_recv.at[0, source]).start()
            else:
                down(source, head - 1, near.at[1, source], near_recv.at[1, source]).start()

    def finish(turn):
        for side in range(2):
            source = pair_at(turn) * 2 + side
            total = part[source, head].astype(jnp.float32)
            for way in range(2):
                up(source, head, near.at[way, source], near_recv.at[way, source]).wait_recv()
                total += near[way, source].astype(jnp.float32)
            done[source] = total.astype(jnp.bfloat16)
            target = rows_ref.at[height // 4, head]
            stays = here & (source == height)

            @pl.when(stays)
            def _():
                pltpu.make_async_copy(done.at[source], target, z_recv).start()

            @pl.when(jnp.logical_not(stays))
            def _():
                remote(
                    done.at[source], target, z_send, z_recv,
                    device_at(column, source, core), lax.rem(height, HEADS),
                ).start()

    for turn in range(10):
        if turn < 8:
            unpack(turn)
        if turn + BACK_AHEAD < 8:
            send_boxes(turn + BACK_AHEAD)
        if 1 <= turn < 9:
            join(turn - 1)
        if turn >= 2:
            finish(turn - 2)
    other = around(head + 1, HEADS)
    remote(sums, sums, sum_send, sum_recv, me, other).wait_recv()
    grand = sums[0]
    for plane in range(1, RING):
        grand += sums[plane]
    means_ref[...] = grand * lax.rsqrt(jnp.mean(grand * grand, axis=1, keepdims=True) + 1e-06)
    lot = boxes_ref.at[pl.ds(0, 56)]
    remote(lot, lot, x_send, x_recv.at[0], me, other).wait_send()
    lot = part.at[pl.ds(0, 12)]
    remote(lot, lot, y_send, far_recv.at[0], me, other).wait_send()

    def sent_sum(index):
        remote(sums.at[0], sums.at[0], sum_send, sum_recv, me, other).wait_send()

    loop(0, RING - jnp.where(owner, 1, 0), sent_sum)

    def sent_rows(index):
        remote(done.at[0], done.at[0], z_send, z_recv, me, other).wait_send()

    loop(0, RING - jnp.where(here, 1, 0), sent_rows)
    remote(rows_ref, rows_ref, z_send, z_recv, me, other).wait_recv()


def collect(boxes, held_notes, sums):
    vmem = pl.BlockSpec(memory_space=pltpu.VMEM)
    dma = pltpu.SemaphoreType.DMA
    return pl.pallas_call(
        collect_kernel,
        out_shape=(
            jax.ShapeDtypeStruct((4, 4, 64, 512), jnp.bfloat16),
            jax.ShapeDtypeStruct(sums.shape[1:], jnp.float32),
        ),
        in_specs=[vmem] * 3,
        out_specs=(vmem,) * 2,
        scratch_shapes=[
            pltpu.VMEM((8, PEERS, 4, 16, 512), jnp.bfloat16),
            pltpu.VMEM((RING, 4, 64, 512), jnp.bfloat16),
            pltpu.VMEM((RING, 64, 512), jnp.bfloat16),
            pltpu.VMEM((2, RING, 64, 512), jnp.bfloat16),
            pltpu.VMEM((RING, 64, 512), jnp.bfloat16),
            pltpu.VMEM((RING,) + sums.shape[1:], jnp.float32),
            dma, dma((8,)), dma((8,)),
            dma, dma((RING,)), dma((2, RING)), dma, dma, dma, dma,
        ],
        compiler_params=pltpu.CompilerParams(
            collective_id=1, has_side_effects=True, vmem_limit_bytes=48 * 2**20
        ),
    )(boxes, held_notes, sums)


def prepare_kernel(
    queries_ref, keys_ref, values_ref, grads_ref, ids_ref, slots_ref, rows_ref, notes_ref, move_sem
):
    head = lax.axis_index("head")
    moves = [
        pltpu.make_async_copy(
            source.at[:, pl.ds(quad * HEAD_DIM, HEAD_DIM)],
            rows_ref.at[quad, :, pl.ds(i * HEAD_DIM, HEAD_DIM)],
            move_sem.at[i, quad],
        )
        for i, source in enumerate((queries_ref, keys_ref, values_ref, grads_ref))
        for quad in range(HEADS)
    ]
    for move in moves:
        move.start()
    count = ids_ref.shape[0]
    copies = 2 * count

    def iota(shape, dim):
        return lax.broadcasted_iota(jnp.int32, shape, dim)

    def ones_where(condition):
        return jnp.where(condition, 1.0, 0.0).astype(jnp.bfloat16)

    square = (count, count)
    unit = ones_where(iota(square, 0) == iota(square, 1))

    def as_row(column_ref):
        turned = product(column_ref[...].astype(jnp.float32).astype(jnp.bfloat16), unit, 0, 0)
        return jnp.concatenate([turned[0:1], turned[1:2]], axis=1)

    ids = as_row(ids_ref).astype(jnp.int32)
    slots = as_row(slots_ref)
    groups = ids // 2
    hit = iota((128, copies), 0) == groups
    before = ones_where(iota((copies, copies), 0) < iota((copies, copies), 1))
    earlier = product(ones_where(hit), before, 1, 0)
    rank = jnp.sum(jnp.where(hit, earlier, 0.0), axis=0, keepdims=True)
    spots = groups * 8 + rank.astype(jnp.int32)
    shape = (PEERS * 128, copies)
    row = iota(shape, 0)
    peer, line = (row // 128, row % 128)
    device = ((peer // 2) * HEADS + head) * 2 + peer % 2
    wanted = jnp.where(line < 32, device * 32 + line, -1)
    kind = iota((8, copies), 0)
    local_ids = (ids % 2).astype(jnp.float32)
    facts = jnp.where(
        kind == 0, slots, jnp.where(kind == 1, local_ids, jnp.where(kind == 2, 1.0, 0.0))
    ).astype(jnp.bfloat16)
    found = product(facts, ones_where(spots == wanted), 1, 1)
    lines = (found[0:1] + CLUSTER_SIZE * found[1:2] + found[2:3] - 1.0).astype(jnp.int32)
    for part in range(4):
        notes_ref[part] = spots[:, part * 128 : (part + 1) * 128]
    for part in range(PEERS):
        notes_ref[4 + part] = lines[:, part * 128 : (part + 1) * 128]
    for move in moves:
        move.wait()


def finish_kernel(rows_ref, means_in_ref, out_ref, query_ref, key_ref, value_ref, means_ref):
    for quad in range(HEADS):
        rows = rows_ref[quad].reshape(256, 512)
        for i, target in enumerate((out_ref, query_ref, key_ref, value_ref)):
            target[:, quad * HEAD_DIM : (quad + 1) * HEAD_DIM] = rows[
                :, i * HEAD_DIM : (i + 1) * HEAD_DIM
            ]
    means_ref[...] = means_in_ref[0:2]


def local(queries, keys, values, out_grad, cluster_ids, slots):
    vmem = pl.BlockSpec(memory_space=pltpu.VMEM)
    params = pltpu.CompilerParams(vmem_limit_bytes=32 * 2**20)
    sent, notes = pl.pallas_call(
        prepare_kernel,
        out_shape=(
            jax.ShapeDtypeStruct((HEADS, 256, 512), jnp.bfloat16),
            jax.ShapeDtypeStruct((4 + PEERS, 1, 128), jnp.int32),
        ),
        in_specs=[pl.BlockSpec(memory_space=pl.ANY)] * 4 + [vmem] * 2,
        out_specs=(vmem,) * 2,
        scratch_shapes=[pltpu.SemaphoreType.DMA((4, HEADS))],
        compiler_params=params,
    )(queries, keys, values, out_grad, cluster_ids, slots)
    arrived, held_notes, held_lines = spread(sent, notes)
    lines_in = (
        held_lines[:, :, 0, :32]
        .reshape(PEERS, RING // 2, 2, 4, 8)
        .transpose(3, 0, 1, 2, 4)
        .reshape(4, 1, 1024)
    )
    boxes, sums = attend_groups(lines_in, arrived)
    rows_back, means = collect(boxes, held_notes, sums)
    whole = jax.ShapeDtypeStruct(queries.shape, jnp.bfloat16)
    return pl.pallas_call(
        finish_kernel,
        out_shape=(whole,) * 4 + (jax.ShapeDtypeStruct((2, HEAD_DIM), jnp.float32),),
        in_specs=[vmem] * 2,
        out_specs=(vmem,) * 5,
        compiler_params=params,
    )(rows_back, means)


def solution(mesh):
    placed = (
        P("seq", "head"),
        P("seq", "head"),
        P("seq", "head"),
        P("seq", "head"),
        P("seq", None),
        P("seq", None),
    )
    return jax.shard_map(
        local,
        mesh=mesh,
        in_specs=placed,
        out_specs=(
            P("seq", "head"),
            P("seq", "head"),
            P("seq", "head"),
            P("seq", "head"),
            P("seq", None),
        ),
        check_vma=False,
    )
```

```python
import functools
import math

import jax
import jax.numpy as jnp
from jax import lax
from jax.experimental import pallas as pl
from jax.experimental.pallas import tpu as pltpu
from jax.sharding import PartitionSpec as P

HEAD_DIM = 128
CLUSTER_SIZE = 256
RING = 16
HEADS = 4
PEERS = 8
MESH = pl.DeviceIdType.MESH
OUTWARD = (0, 1, -1, 2, -2, 3, -3, 4)
RETURN = (4, 3, -2, -3, 2, 1, 0, -1)
AHEAD = 4
BACK_AHEAD = 8


def place():
    me = lax.axis_index("seq")
    head = lax.axis_index("head")
    return (me, head, me // (2 * RING), lax.rem(me // 2, RING), lax.rem(me, 2))


def device_at(column, height, core):
    return (column * RING + height) * 2 + core


def around(value, size):
    return lax.rem(value + size, size)


def signal(barrier, seq, head):
    pl.semaphore_signal(barrier, inc=1, device_id=(seq, head), device_id_type=MESH)


def remote(source, target, send_sem, recv_sem, seq, head):
    return pltpu.make_async_remote_copy(
        src_ref=source,
        dst_ref=target,
        send_sem=send_sem,
        recv_sem=recv_sem,
        device_id=(seq, head),
        device_id_type=MESH,
    )


def loop(first, last, body):
    def step(index, carry):
        body(index)
        return carry

    lax.fori_loop(first, last, step, 0)


def hit_table(notes_ref, pair, head):
    shape = (512, 512)
    row = lax.broadcasted_iota(jnp.int32, shape, 0)
    lane = lax.broadcasted_iota(jnp.int32, shape, 1)
    peer = row // 64
    device = ((peer // 2) * HEADS + head) * 2 + peer % 2
    wanted = (device * 4 + row // 16 % 4) * 8 + row % 8
    copies = [
        jnp.concatenate(
            [notes_ref[pair * 2 + side, 2 * c + part] for side in range(2) for part in range(2)],
            axis=1,
        )
        for c in range(2)
    ]
    hit = (copies[0] == wanted) | (copies[1] == wanted)
    same = row // 8 % 2 == lane // 256
    return jnp.where(hit & same, 1.0, 0.0).astype(jnp.bfloat16)


def spread_kernel(
    rows_ref, notes_ref, boxes_ref, held_notes_ref, lines_ref,
    spread_rows, full, packed, note_send, note_recv, line_send, line_recv, line_own,
    first_send, first_recv, stay_sem, z_send, z_recv, y_send, y_recv, x_send, x_recv, own_sem,
):
    me, head, column, height, core = place()
    mine = column * 2 + core
    barrier = pltpu.get_barrier_semaphore()

    def greet_ring(step):
        signal(barrier, device_at(column, lax.rem(height + step, RING), core), head)

    loop(1, RING, greet_ring)

    def greet_peer(step):
        peer = lax.rem(mine + step, PEERS)
        signal(barrier, device_at(peer // 2, height, lax.rem(peer, 2)), head)

    loop(1, PEERS, greet_peer)
    for step in range(1, HEADS):
        signal(barrier, me, lax.rem(head + step, HEADS))
    other = lax.rem(head + 1, HEADS)
    held_notes_ref[height] = notes_ref[...]
    pl.semaphore_wait(barrier, RING - 1 + PEERS - 1 + HEADS - 1)

    def send_notes(step):
        peer = device_at(column, lax.rem(height + step, RING), core)
        remote(notes_ref, held_notes_ref.at[height], note_send, note_recv, peer, head).start()

    def first_copy(quad, step):
        there = lax.rem(head + step, HEADS)
        return remote(
            rows_ref.at[quad, pl.ds(pl.multiple_of(there * 64, 64), 64)],
            spread_rows.at[head, quad],
            first_send,
            first_recv.at[head, quad],
            me,
            there,
        )

    for step in (0, 3, 2, 1):
        quad = lax.rem(height // 4 + step, 4)
        for way in range(1, HEADS):
            first_copy(quad, way).start()
        own = rows_ref.at[quad, pl.ds(pl.multiple_of(head * 64, 64), 64)]
        pltpu.make_async_copy(own, spread_rows.at[head, quad], first_recv.at[head, quad]).start()

    def stay_copy():
        return pltpu.make_async_copy(
            spread_rows.at[lax.rem(height, HEADS), height // 4], full.at[height, head], stay_sem
        )

    def send_quarters(turn):
        there = lax.rem(height // 2 - OUTWARD[turn] + 8, 8)

        def send_quarter(side):
            plane = there * 2 + side
            row_head, quad = (lax.rem(plane, HEADS), plane // 4)
            source = spread_rows.at[row_head, quad]
            pltpu.make_async_copy(source, source, first_recv.at[row_head, quad]).wait()

            @pl.when(plane == height)
            def _():
                stay_copy().start()

            @pl.when(plane != height)
            def _():
                remote(
                    source, full.at[height, head], z_send, z_recv.at[height],
                    device_at(column, plane, core), head,
                ).start()

        loop(0, 2, send_quarter)

    for turn in range(AHEAD):
        send_quarters(turn)
    loop(1, RING, send_notes)

    def y_copy(source, quarter, step, kind):
        part = full.at[source, around(quarter, HEADS)]
        return remote(
            part, part, y_send, y_recv.at[kind, source], me, around(head + step, HEADS)
        )

    def pair_at(turn):
        return lax.rem(height // 2 + OUTWARD[turn] + 8, 8)

    def share(turn):
        for side in range(2):
            source = pair_at(turn) * 2 + side
            part = full.at[source, head]

            @pl.when(source == height)
            def _():
                stay_copy().wait()

            @pl.when(source != height)
            def _():
                remote(part, part, z_send, z_recv.at[source], me, other).wait_recv()

            y_copy(source, head, 1, 0).start()
            y_copy(source, head, -1, 1).start()

    def relay(turn):
        for side in range(2):
            source = pair_at(turn) * 2 + side
            if side == 0:
                y_copy(source, head - 1, 1, 0).wait_recv()
                y_copy(source, head - 1, 1, 2).start()
                y_copy(source, head + 1, -1, 1).wait_recv()
            else:
                y_copy(source, head + 1, -1, 1).wait_recv()
                y_copy(source, head + 1, -1, 2).start()
                y_copy(source, head - 1, 1, 0).wait_recv()

    def deliver(turn):
        pair = pair_at(turn)
        for side in range(2):
            y_copy(pair * 2 + side, head + 2, 1, 2).wait_recv()
        table = hit_table(held_notes_ref, pair, head)
        tokens = full[pl.ds(pair * 2, 2)].reshape(512, 512)
        result = jnp.dot(table, tokens, preferred_element_type=jnp.float32)
        packed[turn] = result.astype(jnp.bfloat16).reshape(PEERS, 4, 16, 512)
        target = boxes_ref.at[mine * 8 + pair]
        pltpu.make_async_copy(packed.at[turn, mine], target, own_sem.at[turn]).start()

        def send(step):
            peer = lax.rem(mine + step, PEERS)
            remote(
                packed.at[turn, peer], target, x_send, x_recv,
                device_at(peer // 2, height, lax.rem(peer, 2)), head,
            ).start()

        loop(1, PEERS, send)

    def send_lines(step):
        peer = lax.rem(mine + step, PEERS)
        remote(
            held_notes_ref.at[pl.ds(0, RING), 4 + peer], lines_ref.at[mine], line_send, line_recv,
            device_at(peer // 2, height, lax.rem(peer, 2)), head,
        ).start()

    own_lines = pltpu.make_async_copy(
        held_notes_ref.at[pl.ds(0, RING), 4 + mine], lines_ref.at[mine], line_own
    )
    for turn in range(10):
        if turn < 8:
            share(turn)
        if 1 <= turn < 9:
            relay(turn - 1)
        if turn == 2:
            lot = held_notes_ref.at[pl.ds(0, RING - 1)]
            remote(lot, lot, note_send, note_recv, me, other).wait()
            own_lines.start()
            loop(1, PEERS, send_lines)
        if turn >= 2:
            deliver(turn - 2)
        if turn + AHEAD < 8:
            send_quarters(turn + AHEAD)
    for turn in range(8):
        pltpu.make_async_copy(
            packed.at[turn, mine], boxes_ref.at[mine * 8 + turn], own_sem.at[turn]
        ).wait()
    lot = boxes_ref.at[pl.ds(0, 56)]
    remote(lot, lot, x_send, x_recv, me, other).wait()
    own_lines.wait()
    lot = lines_ref.at[pl.ds(0, PEERS - 1)]
    remote(lot, lot, line_send, line_recv, me, other).wait()
    lot = full.at[pl.ds(0, 12)]
    remote(lot, lot, y_send, y_recv.at[0, 0], me, other).wait_send()

    def sent_quarter(index):
        part = full.at[0, 0]
        remote(part, part, z_send, z_recv.at[0], me, other).wait_send()

    loop(0, RING - 1, sent_quarter)
    lot = spread_rows.at[pl.ds(0, HEADS - 1)]
    remote(lot, lot, first_send, first_recv.at[0, 0], me, other).wait_send()


def spread(rows, notes):
    vmem = pl.BlockSpec(memory_space=pltpu.VMEM)
    dma = pltpu.SemaphoreType.DMA
    return pl.pallas_call(
        spread_kernel,
        out_shape=(
            jax.ShapeDtypeStruct((64, 4, 16, 512), jnp.bfloat16),
            jax.ShapeDtypeStruct((RING,) + notes.shape, jnp.int32),
            jax.ShapeDtypeStruct((PEERS, RING) + notes.shape[1:], jnp.int32),
        ),
        in_specs=[vmem] * 2,
        out_specs=(vmem,) * 3,
        scratch_shapes=[
            pltpu.VMEM((HEADS, 4, 64, 512), jnp.bfloat16),
            pltpu.VMEM((RING, 4, 64, 512), jnp.bfloat16),
            pltpu.VMEM((8, PEERS, 4, 16, 512), jnp.bfloat16),
            dma, dma, dma, dma, dma,
            dma, dma((HEADS, 4)), dma,
            dma, dma((RING,)), dma, dma((3, RING)), dma, dma, dma((8,)),
        ],
        compiler_params=pltpu.CompilerParams(
            collective_id=0, has_side_effects=True, vmem_limit_bytes=48 * 2**20
        ),
    )(rows, notes)


def product(left, right, left_dim, right_dim):
    return lax.dot_general(
        left, right, (((left_dim,), (right_dim,)), ((), ())), preferred_element_type=jnp.float32
    )


def attend_kernel(lines_ref, rows_ref, boxes_ref, sums_ref, results):
    scale = 1.0 / math.sqrt(HEAD_DIM)
    shape = (512, 1024)
    row = lax.broadcasted_iota(jnp.int32, shape, 0)
    table = jnp.where(lines_ref[0] == row, 1.0, 0.0).astype(jnp.bfloat16)
    grouped = product(table, rows_ref[...].reshape(1024, 512), 1, 0).astype(jnp.bfloat16)
    size = (CLUSTER_SIZE, CLUSTER_SIZE)
    allowed = lax.broadcasted_iota(jnp.int32, size, 1) <= lax.broadcasted_iota(jnp.int32, size, 0)
    sums_ref[...] = jnp.zeros_like(sums_ref)
    for cluster in range(2):
        first = cluster * CLUSTER_SIZE
        query, key, value, grad = (
            grouped[first : first + CLUSTER_SIZE, i * HEAD_DIM : (i + 1) * HEAD_DIM]
            for i in range(4)
        )
        scores = jnp.where(allowed, product(query, key, 1, 1) * scale, jnp.float32(-1e30))
        weights = jnp.exp(scores - jnp.max(scores, axis=1, keepdims=True))
        attention = weights / jnp.sum(weights, axis=1, keepdims=True)
        attn_low = attention.astype(jnp.bfloat16)
        prob_grad = product(grad, value, 1, 1)
        row_dot = jnp.sum(attention * prob_grad, axis=1, keepdims=True)
        grad_score = (attention * (prob_grad - row_dot) * scale).astype(jnp.bfloat16)
        outs = (
            product(attn_low, value, 1, 0),
            product(grad_score, key, 1, 0),
            product(grad_score, query, 0, 0),
            product(attn_low, grad, 0, 0),
        )
        for i, out in enumerate(outs):
            results[first : first + CLUSTER_SIZE, i * HEAD_DIM : (i + 1) * HEAD_DIM] = out.astype(
                jnp.bfloat16
            )
        key_float = key.astype(jnp.float32)
        normed = key_float * lax.rsqrt(
            jnp.mean(key_float * key_float, axis=1, keepdims=True) + 1e-06
        )
        sums_ref[0, cluster : cluster + 1] = jnp.sum(normed, axis=0, keepdims=True)
    boxes = product(table, results[...], 0, 0)
    boxes_ref[...] = boxes.astype(jnp.bfloat16).reshape(64, 1, 16, 512)


def attend_groups(lines, boxes):
    box_spec = pl.BlockSpec((64, 1, 16, 512), lambda group: (0, group, 0, 0))
    return pl.pallas_call(
        attend_kernel,
        grid=(4,),
        out_shape=(
            jax.ShapeDtypeStruct(boxes.shape, jnp.bfloat16),
            jax.ShapeDtypeStruct((4, 8, HEAD_DIM), jnp.float32),
        ),
        in_specs=[pl.BlockSpec((1, 1, 1024), lambda group: (group, 0, 0)), box_spec],
        out_specs=(box_spec, pl.BlockSpec((1, 8, HEAD_DIM), lambda group: (group, 0, 0))),
        scratch_shapes=[pltpu.VMEM((512, 512), jnp.bfloat16)],
        compiler_params=pltpu.CompilerParams(vmem_limit_bytes=48 * 2**20),
    )(lines, boxes)


def collect_kernel(
    boxes_ref, held_notes_ref, sums_ref, rows_ref, means_ref,
    held, part, far, near, done, sums, x_send, x_recv, own_sem,
    y_send, far_recv, near_recv, z_send, z_recv, sum_send, sum_recv,
):
    me, head, column, height, core = place()
    mine = column * 2 + core
    here = lax.rem(height, HEADS) == head
    owner = (height // 4 == head) & (lax.rem(height // 2, 2) == core)
    barrier = pltpu.get_barrier_semaphore()

    def greet_peer(step):
        peer = lax.rem(mine + step, PEERS)
        signal(barrier, device_at(peer // 2, height, lax.rem(peer, 2)), head)

    loop(1, PEERS, greet_peer)
    for step in (1, HEADS - 1):
        signal(barrier, me, lax.rem(head + step, HEADS))

    def greet_relay(index):
        plane = index // 4 * 4 + head
        quarter = lax.rem(index, 4)

        @pl.when(jnp.logical_not((plane == height) & (quarter == head)))
        def _():
            signal(barrier, device_at(column, plane, core), quarter)

    loop(0, RING, greet_relay)

    def greet_summer(plane):
        @pl.when(jnp.logical_not(owner & (plane == height)))
        def _():
            signal(barrier, device_at(column, plane, lax.rem(height // 2, 2)), height // 4)

    loop(0, RING, greet_summer)
    pl.semaphore_wait(
        barrier, PEERS - 1 + 2 + 2 * RING - jnp.where(here, 1, 0) - jnp.where(owner, 1, 0)
    )

    def pair_at(turn):
        return lax.rem(height // 2 + RETURN[turn] + 8, 8)

    def send_boxes(turn):
        pair = pair_at(turn)
        pltpu.make_async_copy(
            boxes_ref.at[mine * 8 + pair], held.at[pair, mine], own_sem.at[turn]
        ).start()

        def send_box(step):
            peer = lax.rem(mine + step, PEERS)
            remote(
                boxes_ref.at[peer * 8 + pair], held.at[pair, mine], x_send, x_recv.at[pair],
                device_at(peer // 2, height, lax.rem(peer, 2)), head,
            ).start()

        loop(1, PEERS, send_box)

    for turn in range(BACK_AHEAD):
        send_boxes(turn)

    def send_sum(index):
        group = index // 4
        there = lax.rem(head + index, HEADS)
        peer = device_at(column, (head * 2 + core) * 2 + group // 2, lax.rem(group, 2))
        stays = (peer == me) & (there == head)

        @pl.when(stays)
        def _():
            pltpu.make_async_copy(sums_ref.at[group], sums.at[height], sum_recv).start()

        @pl.when(jnp.logical_not(stays))
        def _():
            remote(
                sums_ref.at[group], sums.at[height], sum_send, sum_recv, peer, there
            ).start()

    loop(0, RING, send_sum)

    def up(source, quarter, target, recv):
        return remote(
            part.at[source, around(quarter, HEADS)], target, y_send, recv, me,
            around(head + 1, HEADS),
        )

    def down(source, quarter, target, recv):
        return remote(
            part.at[source, around(quarter, HEADS)], target, y_send, recv, me,
            around(head - 1, HEADS),
        )

    def unpack(turn):
        pair = pair_at(turn)
        pltpu.make_async_copy(
            boxes_ref.at[mine * 8 + pair], held.at[pair, mine], own_sem.at[turn]
        ).wait()
        lot = held.at[pair, pl.ds(0, PEERS - 1)]
        remote(lot, lot, x_send, x_recv.at[pair], me, around(head + 1, HEADS)).wait_recv()
        table = hit_table(held_notes_ref, pair, head)
        result = lax.dot_general(
            table, held[pair].reshape(512, 512), (((0,), (0,)), ((), ())),
            preferred_element_type=jnp.float32,
        )
        part[pl.ds(pair * 2, 2)] = result.astype(jnp.bfloat16).reshape(2, 4, 64, 512)
        even, odd = (pair * 2, pair * 2 + 1)
        up(even, head + 2, far.at[even], far_recv.at[even]).start()
        down(even, head - 1, near.at[1, even], near_recv.at[1, even]).start()
        down(odd, head + 2, far.at[odd], far_recv.at[odd]).start()
        up(odd, head + 1, near.at[0, odd], near_recv.at[0, odd]).start()

    def join(turn):
        even = pair_at(turn) * 2
        for source, step in ((even, 1), (even + 1, -1)):
            spot = around(head + step, HEADS)
            up(source, head + step, far.at[source], far_recv.at[source]).wait_recv()
            total = part[source, spot].astype(jnp.float32) + far[source].astype(jnp.float32)
            part[source, spot] = total.astype(jnp.bfloat16)
            if step == 1:
                up(source, head + 1, near.at[0, source], near_recv.at[0, source]).start()
            else:
                down(source, head - 1, near.at[1, source], near_recv.at[1, source]).start()

    def finish(turn):
        for side in range(2):
            source = pair_at(turn) * 2 + side
            total = part[source, head].astype(jnp.float32)
            for way in range(2):
                up(source, head, near.at[way, source], near_recv.at[way, source]).wait_recv()
                total += near[way, source].astype(jnp.float32)
            done[source] = total.astype(jnp.bfloat16)
            target = rows_ref.at[height // 4, head]
            stays = here & (source == height)

            @pl.when(stays)
            def _():
                pltpu.make_async_copy(done.at[source], target, z_recv).start()

            @pl.when(jnp.logical_not(stays))
            def _():
                remote(
                    done.at[source], target, z_send, z_recv,
                    device_at(column, source, core), lax.rem(height, HEADS),
                ).start()

    for turn in range(10):
        if turn < 8:
            unpack(turn)
        if turn + BACK_AHEAD < 8:
            send_boxes(turn + BACK_AHEAD)
        if 1 <= turn < 9:
            join(turn - 1)
        if turn >= 2:
            finish(turn - 2)
    other = around(head + 1, HEADS)
    remote(sums, sums, sum_send, sum_recv, me, other).wait_recv()
    grand = sums[0]
    for plane in range(1, RING):
        grand += sums[plane]
    means_ref[...] = grand * lax.rsqrt(jnp.mean(grand * grand, axis=1, keepdims=True) + 1e-06)
    lot = boxes_ref.at[pl.ds(0, 56)]
    remote(lot, lot, x_send, x_recv.at[0], me, other).wait_send()
    lot = part.at[pl.ds(0, 12)]
    remote(lot, lot, y_send, far_recv.at[0], me, other).wait_send()

    def sent_sum(index):
        remote(sums.at[0], sums.at[0], sum_send, sum_recv, me, other).wait_send()

    loop(0, RING - jnp.where(owner, 1, 0), sent_sum)

    def sent_rows(index):
        remote(done.at[0], done.at[0], z_send, z_recv, me, other).wait_send()

    loop(0, RING - jnp.where(here, 1, 0), sent_rows)
    remote(rows_ref, rows_ref, z_send, z_recv, me, other).wait_recv()


def collect(boxes, held_notes, sums):
    vmem = pl.BlockSpec(memory_space=pltpu.VMEM)
    dma = pltpu.SemaphoreType.DMA
    return pl.pallas_call(
        collect_kernel,
        out_shape=(
            jax.ShapeDtypeStruct((4, 4, 64, 512), jnp.bfloat16),
            jax.ShapeDtypeStruct(sums.shape[1:], jnp.float32),
        ),
        in_specs=[vmem] * 3,
        out_specs=(vmem,) * 2,
        scratch_shapes=[
            pltpu.VMEM((8, PEERS, 4, 16, 512), jnp.bfloat16),
            pltpu.VMEM((RING, 4, 64, 512), jnp.bfloat16),
            pltpu.VMEM((RING, 64, 512), jnp.bfloat16),
            pltpu.VMEM((2, RING, 64, 512), jnp.bfloat16),
            pltpu.VMEM((RING, 64, 512), jnp.bfloat16),
            pltpu.VMEM((RING,) + sums.shape[1:], jnp.float32),
            dma, dma((8,)), dma((8,)),
            dma, dma((RING,)), dma((2, RING)), dma, dma, dma, dma,
        ],
        compiler_params=pltpu.CompilerParams(
            collective_id=1, has_side_effects=True, vmem_limit_bytes=48 * 2**20
        ),
    )(boxes, held_notes, sums)


def prepare_kernel(
    queries_ref, keys_ref, values_ref, grads_ref, ids_ref, slots_ref, rows_ref, notes_ref, move_sem
):
    head = lax.axis_index("head")
    moves = [
        pltpu.make_async_copy(
            source.at[:, pl.ds(quad * HEAD_DIM, HEAD_DIM)],
            rows_ref.at[quad, :, pl.ds(i * HEAD_DIM, HEAD_DIM)],
            move_sem.at[i, quad],
        )
        for i, source in enumerate((queries_ref, keys_ref, values_ref, grads_ref))
        for quad in range(HEADS)
    ]
    for move in moves:
        move.start()
    count = ids_ref.shape[0]
    copies = 2 * count

    def iota(shape, dim):
        return lax.broadcasted_iota(jnp.int32, shape, dim)

    def ones_where(condition):
        return jnp.where(condition, 1.0, 0.0).astype(jnp.bfloat16)

    square = (count, count)
    unit = ones_where(iota(square, 0) == iota(square, 1))

    def as_row(column_ref):
        turned = product(column_ref[...].astype(jnp.float32).astype(jnp.bfloat16), unit, 0, 0)
        return jnp.concatenate([turned[0:1], turned[1:2]], axis=1)

    ids = as_row(ids_ref).astype(jnp.int32)
    slots = as_row(slots_ref)
    groups = ids // 2
    hit = iota((128, copies), 0) == groups
    before = ones_where(iota((copies, copies), 0) < iota((copies, copies), 1))
    earlier = product(ones_where(hit), before, 1, 0)
    rank = jnp.sum(jnp.where(hit, earlier, 0.0), axis=0, keepdims=True)
    spots = groups * 8 + rank.astype(jnp.int32)
    shape = (PEERS * 128, copies)
    row = iota(shape, 0)
    peer, line = (row // 128, row % 128)
    device = ((peer // 2) * HEADS + head) * 2 + peer % 2
    wanted = jnp.where(line < 32, device * 32 + line, -1)
    kind = iota((8, copies), 0)
    local_ids = (ids % 2).astype(jnp.float32)
    facts = jnp.where(
        kind == 0, slots, jnp.where(kind == 1, local_ids, jnp.where(kind == 2, 1.0, 0.0))
    ).astype(jnp.bfloat16)
    found = product(facts, ones_where(spots == wanted), 1, 1)
    lines = (found[0:1] + CLUSTER_SIZE * found[1:2] + found[2:3] - 1.0).astype(jnp.int32)
    for part in range(4):
        notes_ref[part] = spots[:, part * 128 : (part + 1) * 128]
    for part in range(PEERS):
        notes_ref[4 + part] = lines[:, part * 128 : (part + 1) * 128]
    for move in moves:
        move.wait()


def finish_kernel(rows_ref, means_in_ref, out_ref, query_ref, key_ref, value_ref, means_ref):
    for quad in range(HEADS):
        rows = rows_ref[quad].reshape(256, 512)
        for i, target in enumerate((out_ref, query_ref, key_ref, value_ref)):
            target[:, quad * HEAD_DIM : (quad + 1) * HEAD_DIM] = rows[
                :, i * HEAD_DIM : (i + 1) * HEAD_DIM
            ]
    means_ref[...] = means_in_ref[0:2]


def local(queries, keys, values, out_grad, cluster_ids, slots):
    vmem = pl.BlockSpec(memory_space=pltpu.VMEM)
    params = pltpu.CompilerParams(vmem_limit_bytes=32 * 2**20)
    sent, notes = pl.pallas_call(
        prepare_kernel,
        out_shape=(
            jax.ShapeDtypeStruct((HEADS, 256, 512), jnp.bfloat16),
            jax.ShapeDtypeStruct((4 + PEERS, 1, 128), jnp.int32),
        ),
        in_specs=[pl.BlockSpec(memory_space=pl.ANY)] * 4 + [vmem] * 2,
        out_specs=(vmem,) * 2,
        scratch_shapes=[pltpu.SemaphoreType.DMA((4, HEADS))],
        compiler_params=pltpu.CompilerParams(vmem_limit_bytes=60 * 2**20),
    )(queries, keys, values, out_grad, cluster_ids, slots)
    arrived, held_notes, held_lines = spread(sent, notes)
    lines_in = (
        held_lines[:, :, 0, :32]
        .reshape(PEERS, RING // 2, 2, 4, 8)
        .transpose(3, 0, 1, 2, 4)
        .reshape(4, 1, 1024)
    )
    boxes, sums = attend_groups(lines_in, arrived)
    rows_back, means = collect(boxes, held_notes, sums)
    whole = jax.ShapeDtypeStruct(queries.shape, jnp.bfloat16)
    return pl.pallas_call(
        finish_kernel,
        out_shape=(whole,) * 4 + (jax.ShapeDtypeStruct((2, HEAD_DIM), jnp.float32),),
        in_specs=[vmem] * 2,
        out_specs=(vmem,) * 5,
        compiler_params=params,
    )(rows_back, means)


def solution(mesh):
    placed = (
        P("seq", "head"),
        P("seq", "head"),
        P("seq", "head"),
        P("seq", "head"),
        P("seq", None),
        P("seq", None),
    )
    return jax.shard_map(
        local,
        mesh=mesh,
        in_specs=placed,
        out_specs=(
            P("seq", "head"),
            P("seq", "head"),
            P("seq", "head"),
            P("seq", "head"),
            P("seq", None),
        ),
        check_vma=False,
    )
```
